128 devices in a mesh: dom: 32 (over y, x, core), rep: 4 (over z).
Axes of the slice: x: 4, y: 4, z: 4, core: 2. Of those that a mesh axis runs over, the one named last changes fastest.
Arguments:
- feature_grid: bfloat16 [32, 32, 32768], P('dom'), may hold values from -6 to 6
- fine_in: bfloat16 [32, 64, 32], P('dom'), may hold values from -1 to 1
- fine_mid: bfloat16 [32, 2, 64, 64], P('dom'), may hold values from -0.75 to 0.75
- fine_out: bfloat16 [32, 64], P('dom'), may hold values from -0.75 to 0.75
- prop_in: bfloat16 [32, 16, 32], P('dom'), may hold values from -1 to 1
- prop_out: bfloat16 [32, 16], P('dom'), may hold values from -1.5 to 1.5
- sample_cells: int32 [32, 4, 32, 2048], P('dom', 'rep'), may hold values from 0 to 31710, as said below
- sample_geometry: bfloat16 [4, 32, 4, 32, 2048], P(None, 'dom', 'rep'), may hold values from 0 to 1, as said below
- slot_ray: int32 [32, 4, 32, 32], P('dom', 'rep'), may hold values from 0 to 255, as said below
- slot_rank: int32 [32, 4, 32, 32], P('dom', 'rep'), may hold values from 0 to 31, as said below
- bucket_count: int32 [32, 4, 32], P('dom', 'rep'), may hold values from 1 to 32, as said below
Outputs:
- ray_loss: float32 [32, 4, 256], P('dom', 'rep')
- prop_in_grad: float32 [32, 16, 32], P('dom')
- prop_out_grad: float32 [32, 16], P('dom')
The draws below stay inside these ranges and needn't reach their ends.
Inputs may be any that keep to these rules, and one draw needn't show every extreme that they name: `sample_cells`: each base cell's three coordinates lie in 0 to 30, so all eight corners are inside the grid. `sample_geometry`: rows 0 to 2 lie in 0 to 1; row 3 is positive. `slot_ray`: within one bucket the rays are distinct. `slot_rank`: live segments of one ray on one device have distinct ranks. `bucket_count`: the live slots of a bucket are its first ones; in every draw one partition receives full buckets from every device.
All inputs are finite; a program needn't handle non-finite values.
Results may differ from the reference program's by a relative error of at most 0.0024.
Values may be sent and summed in bfloat16 or wider, within the bound.
A program may use at most 192 MiB of HBM per device.

```python
import math
import jax
import jax.numpy as jnp
from jax import lax

S = 64
GR = 32
F = 32
FH = 64
MIDS = 2
PH = 16
CAP = 32
RAY_DEV = 256
N_DOM = 32
N_REP = 4


def draw_sample_cells(key, part):
    array_shape = (N_DOM, N_REP, N_DOM, CAP * S)
    coord_x = jax.random.randint(jax.random.fold_in(key, 1), array_shape, 0, GR - 1)
    coord_y = jax.random.randint(jax.random.fold_in(key, 2), array_shape, 0, GR - 1)
    coord_z = jax.random.randint(jax.random.fold_in(key, 3), array_shape, 0, GR - 1)
    return ((coord_x * GR + coord_y) * GR + coord_z).astype(jnp.int32)


def draw_sample_geometry(key, part):
    array_shape = (N_DOM, N_REP, N_DOM, CAP * S)
    offsets = jax.random.uniform(jax.random.fold_in(key, 4), (3,) + array_shape, jnp.float32)
    lowest, highest = (0.004, 0.02)
    spacing = jnp.exp(jax.random.uniform(jax.random.fold_in(key, 5), (1,) + array_shape, jnp.float32, math.log(lowest), math.log(highest)))
    return jnp.concatenate([offsets, spacing], axis=0).astype(jnp.bfloat16)


def segment_plan(key):
    heaviest = jax.random.randint(jax.random.fold_in(key, 11), (), 0, N_DOM)
    counts = jax.random.randint(jax.random.fold_in(key, 12), (N_DOM, N_REP, N_DOM), 1, max(2, 5 * CAP // 8))
    column = jnp.arange(N_DOM)[None, None, :]
    counts = jnp.where(column == heaviest, CAP, counts).astype(jnp.int32)
    scores = jax.random.randint(jax.random.fold_in(key, 13), (N_DOM, N_REP, N_DOM, RAY_DEV), 0, 2 ** 20) * RAY_DEV + jnp.arange(RAY_DEV)
    ray_ids = jnp.argsort(scores, axis=-1)[..., :CAP].astype(jnp.int32)
    shifts = jax.random.randint(jax.random.fold_in(key, 14), (N_DOM, N_REP, 1, RAY_DEV), 0, N_DOM)
    shifts = jnp.broadcast_to(shifts, (N_DOM, N_REP, N_DOM, RAY_DEV))
    rank_ids = (jnp.take_along_axis(shifts, ray_ids, axis=-1) + column[..., None]) % N_DOM
    return (ray_ids, rank_ids.astype(jnp.int32), counts)


def draw_slot_ray(key, part):
    return segment_plan(key)[0]


def draw_slot_rank(key, part):
    return segment_plan(key)[1]


def draw_bucket_count(key, part):
    return segment_plan(key)[2]


def shard_levels(stream_key, dims, cuts, smallest, high):
    level, own = 1.0, jax.random.fold_in(stream_key, 6)
    for dim, blocks in cuts:
        heights = jnp.exp(jax.random.uniform(jax.random.fold_in(own, dim), (blocks,), jnp.float32, smallest / len(cuts), high / len(cuts)))
        level = level * jnp.repeat(heights, dims[dim] // blocks).reshape([-1 if axis == dim else 1 for axis in range(len(dims))])
    return level


def noise(own_key, extent, scale, reach, split=(), held_as=jnp.bfloat16):
    entries = scale * jax.random.normal(own_key, extent, jnp.float32)
    if split:
        entries = entries * shard_levels(own_key, extent, split, -0.22, 0.18)
    return jnp.clip(entries, -reach, reach).astype(held_as)


def setup_inputs(seed: int = 0) -> dict:
    keys = jax.random.split(jax.random.key(seed), 12)
    feature_grid = noise(keys[0], (N_DOM, F, GR ** 3), 1.0, 6.0, ((0, 32),))
    fine_in = noise(keys[1], (N_DOM, FH, F), F ** -0.5, 1.0, ((0, 32),))
    fine_mid = noise(keys[2], (N_DOM, MIDS, FH, FH), FH ** -0.5, 0.75, ((0, 32),))
    fine_out = noise(keys[3], (N_DOM, FH), FH ** -0.5, 0.75, ((0, 32),))
    prop_in = noise(keys[4], (N_DOM, PH, F), F ** -0.5, 1.0, ((0, 32),))
    prop_out = noise(keys[5], (N_DOM, PH), PH ** -0.5, 1.5, ((0, 32),))
    sample_cells = draw_sample_cells(jax.random.fold_in(keys[11], 71), 0)
    sample_geometry = draw_sample_geometry(jax.random.fold_in(keys[11], 71), 0)
    slot_ray = draw_slot_ray(jax.random.fold_in(keys[11], 71), 0)
    slot_rank = draw_slot_rank(jax.random.fold_in(keys[11], 71), 0)
    bucket_count = draw_bucket_count(jax.random.fold_in(keys[11], 71), 0)
    return {"feature_grid": feature_grid, "fine_in": fine_in, "fine_mid": fine_mid, "fine_out": fine_out, "prop_in": prop_in, "prop_out": prop_out, "sample_cells": sample_cells, "sample_geometry": sample_geometry, "slot_ray": slot_ray, "slot_rank": slot_rank, "bucket_count": bucket_count}


distill_weight = 50.0

def interpolate(feature_grid, cell_index, geometry):
    offsets = geometry[:3].astype(jnp.float32)
    summed = jnp.zeros((feature_grid.shape[0], cell_index.shape[0]), jnp.float32)
    for corner in range(8):
        step_x = corner // 4
        step_y = corner // 2 % 2
        step_z = corner % 2
        shifted = cell_index + (step_x * GR + step_y) * GR + step_z
        factor = (offsets[0] if step_x else 1.0 - offsets[0]) * (offsets[1] if step_y else 1.0 - offsets[1]) * (offsets[2] if step_z else 1.0 - offsets[2])
        summed = summed + jnp.take(feature_grid, shifted, axis=1).astype(jnp.float32) * factor
    return summed.astype(jnp.bfloat16)

def fine_density(fine_in, fine_mid, fine_out, features):
    hidden_units = jax.nn.relu(jnp.dot(fine_in, features, preferred_element_type=jnp.float32)).astype(jnp.bfloat16)
    for layer_index in range(fine_mid.shape[0]):
        hidden_units = jax.nn.relu(jnp.dot(fine_mid[layer_index], hidden_units, preferred_element_type=jnp.float32)).astype(jnp.bfloat16)
    return jax.nn.softplus(jnp.dot(fine_out, hidden_units, preferred_element_type=jnp.float32))

def proposal_parts(prop_in, prop_out, features):
    pre_hidden = jnp.dot(prop_in, features, preferred_element_type=jnp.float32)
    hidden_units = jax.nn.relu(pre_hidden).astype(jnp.bfloat16)
    logits = jnp.dot(prop_out, hidden_units, preferred_element_type=jnp.float32)
    return (pre_hidden, hidden_units, logits)

def proposal_grads(prop_in, prop_out, features, sigma_grad):
    pre_hidden, hidden_units, logits = proposal_parts(prop_in, prop_out, features)
    logit_grad = (sigma_grad * jax.nn.sigmoid(logits)).astype(jnp.bfloat16)
    out_grad = jnp.dot(hidden_units, logit_grad, preferred_element_type=jnp.float32)
    spread = prop_out[:, None].astype(jnp.float32) * logit_grad[None, :].astype(jnp.float32)
    hidden_grad = jnp.where(pre_hidden > 0, spread, jnp.float32(0.0)).astype(jnp.bfloat16)
    in_grad = lax.dot_general(hidden_grad, features, (((1,), (1,)), ((), ())), preferred_element_type=jnp.float32)
    return (in_grad, out_grad)

def absorbed(sigma, spacing):
    optical = sigma * spacing
    depth_sum = jnp.cumsum(optical, axis=-2)
    return (jnp.exp(optical - depth_sum) - jnp.exp(-depth_sum), -depth_sum[..., -1, :])

def proposal_terms(sigma, fine_absorbed, spacing):
    prop_absorbed, log_prop = absorbed(sigma, spacing)
    return (lax.optimization_barrier(jnp.sum(prop_absorbed * prop_absorbed, axis=-2)), lax.optimization_barrier(jnp.sum(prop_absorbed * fine_absorbed, axis=-2)), log_prop)

def segment_stats(prop_sigma, fine_sigma, spacing):
    fine_absorbed, log_fine = absorbed(fine_sigma, spacing)
    sum_aa, sum_ab, log_prop = proposal_terms(prop_sigma, fine_absorbed, spacing)
    sum_bb = lax.optimization_barrier(jnp.sum(fine_absorbed * fine_absorbed, axis=-2))
    return (log_prop, log_fine, sum_aa, sum_ab, sum_bb)

def spread_sum(values, ray_table, rank_table, matrix):
    per_ray = lax.dot_general(ray_table, rank_table * values[None, :], (((1,), (1,)), ((), ())), precision=lax.Precision.HIGHEST)
    per_ray = jnp.dot(per_ray, matrix, precision=lax.Precision.HIGHEST)
    spread = lax.dot_general(per_ray, ray_table, (((0,), (0,)), ((), ())), precision=lax.Precision.HIGHEST)
    return lax.optimization_barrier(jnp.sum(spread * rank_table, axis=0))

def ray_side(log_prop, log_fine, sum_aa, sum_ab, sum_bb, ray_ids, rank_ids, counts):
    part_count, capacity = ray_ids.shape
    live_mask = (jnp.arange(capacity)[None, :] < counts[:, None]).astype(jnp.float32).reshape(-1)
    ray_flat = ray_ids.reshape(-1)
    rank_flat = rank_ids.reshape(-1)
    ray_table = (jnp.arange(RAY_DEV)[:, None] == ray_flat[None, :]).astype(jnp.float32)
    rank_table = (jnp.arange(part_count)[:, None] == rank_flat[None, :]).astype(jnp.float32)
    later = (jnp.arange(part_count)[:, None] < jnp.arange(part_count)[None, :]).astype(jnp.float32)
    entry_prop = jnp.exp(spread_sum(log_prop.reshape(-1) * live_mask, ray_table, rank_table, later)) * live_mask
    entry_fine = jnp.exp(spread_sum(log_fine.reshape(-1) * live_mask, ray_table, rank_table, later)) * live_mask
    flat_aa = sum_aa.reshape(-1)
    flat_ab = sum_ab.reshape(-1)
    flat_bb = sum_bb.reshape(-1)
    seg_loss = entry_prop * entry_prop * flat_aa - 2.0 * entry_prop * entry_fine * flat_ab + entry_fine * entry_fine * flat_bb
    slot_grad = distill_weight * (entry_prop * flat_aa - entry_fine * flat_ab) * entry_prop
    carried = spread_sum(slot_grad, ray_table, rank_table, later.T) * live_mask
    ray_loss = 0.5 * distill_weight * jnp.dot(ray_table, seg_loss, precision=lax.Precision.HIGHEST)
    coef_aa = 0.5 * distill_weight * entry_prop * entry_prop
    coef_ab = -distill_weight * entry_prop * entry_fine
    return (jnp.stack([coef_aa, coef_ab, carried]).reshape(3, part_count, capacity), ray_loss)

def reference(feature_grid, fine_in, fine_mid, fine_out, prop_in, prop_out, sample_cells, sample_geometry, slot_ray, slot_rank, bucket_count):
    owner_geometry = jnp.transpose(sample_geometry, (0, 3, 2, 1, 4))
    owners = jnp.arange(N_DOM * N_REP, dtype=jnp.int32)

    def owner_inputs(owner_index):
        part_id = owner_index // N_REP
        replica = owner_index % N_REP
        cell_index = sample_cells[part_id, replica].reshape(-1)
        geometry = owner_geometry[:, part_id, replica].reshape(4, -1)
        features = interpolate(feature_grid[part_id], cell_index, geometry)
        spacing = geometry[3].astype(jnp.float32).reshape(N_DOM, S, CAP)
        return (part_id, features, spacing)

    def owner_forward(owner_index):
        part_id, features, spacing = owner_inputs(owner_index)
        fine_sigma = fine_density(fine_in[part_id], fine_mid[part_id], fine_out[part_id], features)
        prop_sigma = jax.nn.softplus(proposal_parts(prop_in[part_id], prop_out[part_id], features)[2])
        stats = segment_stats(prop_sigma.reshape(N_DOM, S, CAP), fine_sigma.reshape(N_DOM, S, CAP), spacing)
        return (jnp.stack(stats), fine_sigma)
    stats, fine_all = lax.map(owner_forward, owners)
    ray_stats = jnp.transpose(stats.reshape(N_DOM, N_REP, 5, N_DOM, CAP), (3, 1, 2, 0, 4)).reshape(N_DOM * N_REP, 5, N_DOM, CAP)

    def ray_device(packed):
        stat_block, ray_ids, rank_ids, counts = packed
        return ray_side(stat_block[0], stat_block[1], stat_block[2], stat_block[3], stat_block[4], ray_ids, rank_ids, counts)
    factors, losses = lax.map(ray_device, (ray_stats, slot_ray.reshape(-1, N_DOM, CAP), slot_rank.reshape(-1, N_DOM, CAP), bucket_count.reshape(-1, N_DOM)))
    owner_factors = jnp.transpose(factors.reshape(N_DOM, N_REP, 3, N_DOM, CAP), (3, 1, 2, 0, 4)).reshape(N_DOM * N_REP, 3, N_DOM, CAP)

    def owner_backward(packed):
        owner_index, fine_sigma, factor = packed
        part_id, features, spacing = owner_inputs(owner_index)
        prop_sigma = jax.nn.softplus(proposal_parts(prop_in[part_id], prop_out[part_id], features)[2])
        fine_absorbed = absorbed(fine_sigma.reshape(N_DOM, S, CAP), spacing)[0]
        terms_value, pullback = jax.vjp(lambda sigma: proposal_terms(sigma, fine_absorbed, spacing), prop_sigma.reshape(N_DOM, S, CAP))
        sigma_grad = pullback((factor[0], factor[1], factor[2]))[0]
        return proposal_grads(prop_in[part_id], prop_out[part_id], features, sigma_grad.reshape(-1))
    in_grads, out_grads = lax.map(owner_backward, (owners, fine_all, owner_factors))
    return (losses.reshape(N_DOM, N_REP, RAY_DEV), in_grads.reshape(N_DOM, N_REP, PH, F).sum(axis=1), out_grads.reshape(N_DOM, N_REP, PH).sum(axis=1))
```

```python
import functools

import jax
import jax.numpy as jnp
from jax import lax
from jax.experimental import pallas as pl
from jax.experimental.pallas import tpu as pltpu
from jax.sharding import PartitionSpec as P

GR = 32
RAY_DEV = 256
TILE = 512

distill_weight = 50.0
f32 = jnp.float32
bf16 = jnp.bfloat16
LANES_BOTH = (((1,), (1,)), ((), ()))


def softplus(x):
    return jnp.maximum(x, 0.0) + jnp.log1p(jnp.exp(-jnp.abs(x)))


def group_total(x):
    once = x + pltpu.roll(x, 32, 1)
    return once + pltpu.roll(once, 64, 1)


def scan_segment(x, rows, forward):
    lane = lax.broadcasted_iota(jnp.int32, x.shape, 1)
    row = lax.broadcasted_iota(jnp.int32, x.shape, 0) % rows
    height = x.shape[0]

    def moved(value, step, axis):
        size = height if axis == 0 else 128
        return pltpu.roll(value, step if forward else size - step, axis)

    within = x
    for step in (32, 64):
        keep = lane >= step if forward else lane < 128 - step
        within = within + jnp.where(keep, moved(within, step, 1), 0.0)
    total = group_total(x)
    running = total
    step = 1
    while step < rows:
        keep = row >= step if forward else row < rows - step
        running = running + jnp.where(keep, moved(running, step, 0), 0.0)
        step *= 2
    edge = row >= 1 if forward else row < rows - 1
    return within + jnp.where(edge, moved(running, 1, 0), 0.0), total


def owner_kernel(
    cells_ref, geom_ref, grid_ref, fine_in_ref, fine_mid_ref, fine_out_ref, prop_in_ref, prop_out_ref,
    kept_ref, back_ref, stats_ref,
    table, even0, even1, odd0, odd1, geo, fine_logit, prop_logit, spacing,
):
    sources, width = cells_ref.shape
    tiles_per = width // TILE
    tile_total = sources * tiles_per
    cell_blocks = grid_ref.shape[1] // 128
    rows_per = width // 128

    geo[...] = geom_ref[...].astype(f32)
    lane = lax.broadcasted_iota(jnp.int32, (GR, 128), 1)

    def build(block, carry):
        here = grid_ref[:, pl.ds(pl.multiple_of(block * 128, 128), 128)].astype(f32)
        after = jnp.minimum(block + 1, cell_blocks - 1)
        there = grid_ref[:, pl.ds(pl.multiple_of(after * 128, 128), 128)].astype(f32)
        pieces = [here]
        for shift in (1, GR, GR + 1):
            pieces.append(
                jnp.where(
                    lane < 128 - shift,
                    pltpu.roll(here, 128 - shift, 1),
                    pltpu.roll(there, 128 - shift, 1),
                )
            )
        table[pl.ds(pl.multiple_of(block * 128, 128), 128), :] = jnp.transpose(
            jnp.concatenate(pieces, axis=0)
        )
        return carry

    lax.fori_loop(0, cell_blocks, build, 0, unroll=2)

    first = jnp.concatenate([fine_in_ref[...], prop_in_ref[...]], axis=0)
    hidden = fine_in_ref.shape[0]
    eye = (
        lax.broadcasted_iota(jnp.int32, (256, 256), 0)
        == lax.broadcasted_iota(jnp.int32, (256, 256), 1)
    ).astype(f32).astype(bf16)

    def gather(tile, low, high):
        source = tile // tiles_per
        base = (tile % tiles_per) * TILE
        for j in range(TILE):
            cell = cells_ref[source, base + j]
            low[pl.ds(j, 1), :] = table[pl.ds(cell, 1), :]
            high[pl.ds(j, 1), :] = table[pl.ds(cell + GR * GR, 1), :]

    def evaluate(tile, low, high):
        source = tile // tiles_per
        lanes = pl.ds(pl.multiple_of((tile % tiles_per) * TILE, TILE), TILE)
        rows = jnp.concatenate([low[...], high[...]], axis=1).astype(bf16)
        turned = lax.dot_general(eye, rows, LANES_BOTH, preferred_element_type=f32)
        offsets = [geo[axis, pl.ds(source, 1), lanes] for axis in range(3)]
        factors = [[1.0 - value, value] for value in offsets]
        summed = jnp.zeros((32, TILE), f32)
        for corner in range(8):
            factor = (
                factors[0][corner // 4] * factors[1][corner // 2 % 2] * factors[2][corner % 2]
            )
            summed = summed + turned[corner * 32 : (corner + 1) * 32] * factor
        features = summed.astype(bf16)
        both = jnp.maximum(jnp.dot(first, features, preferred_element_type=f32), 0.0).astype(bf16)
        prop_hidden = both[hidden:]
        fine_hidden = both[:hidden]
        kept_ref[source, pl.ds(0, 32), lanes] = features
        kept_ref[source, pl.ds(32, 16), lanes] = prop_hidden
        for layer in range(fine_mid_ref.shape[0]):
            fine_hidden = jnp.maximum(
                jnp.dot(fine_mid_ref[layer], fine_hidden, preferred_element_type=f32), 0.0
            ).astype(bf16)
        fine = jnp.dot(fine_out_ref[...], fine_hidden, preferred_element_type=f32)
        prop = jnp.dot(prop_out_ref[...], prop_hidden, preferred_element_type=f32)
        step = geo[3, pl.ds(source, 1), lanes]
        for part in range(TILE // 128):
            row = pl.ds(tile * (TILE // 128) + part, 1)
            cut = slice(part * 128, (part + 1) * 128)
            fine_logit[row, :] = fine[:, cut]
            prop_logit[row, :] = prop[:, cut]
            spacing[row, :] = step[:, cut]

    gather(0, even0, even1)

    def pair(index, carry):
        tile = index * 2
        gather(tile + 1, odd0, odd1)
        evaluate(tile, even0, even1)
        gather(jnp.minimum(tile + 2, tile_total - 1), even0, even1)
        evaluate(tile + 1, odd0, odd1)
        return carry

    lax.fori_loop(0, tile_total // 2, pair, 0)

    gap = spacing[...]
    prop_raw = prop_logit[...]
    optical = softplus(prop_raw) * gap
    depth, prop_total = scan_segment(optical, rows_per, True)
    before = jnp.exp(optical - depth)
    prop_taken = before - jnp.exp(-depth)
    back_ref[0] = prop_taken
    back_ref[1] = before
    back_ref[2] = gap * jax.nn.sigmoid(prop_raw)
    fine_optical = softplus(fine_logit[...]) * gap
    fine_depth, fine_total = scan_segment(fine_optical, rows_per, True)
    fine_taken = jnp.exp(fine_optical - fine_depth) - jnp.exp(-fine_depth)
    back_ref[3] = fine_taken

    def per_segment(value, totalled):
        over_rows = jnp.sum(value.reshape(sources, rows_per, 128), axis=1)
        return over_rows if totalled else group_total(over_rows)

    sum_aa = per_segment(prop_taken * prop_taken, False)
    sum_ab = per_segment(prop_taken * fine_taken, False)
    sum_bb = per_segment(fine_taken * fine_taken, False)
    log_prop = -per_segment(prop_total, True)
    log_fine = -per_segment(fine_total, True)
    part = lax.broadcasted_iota(jnp.int32, (sources, 128), 1) // 32
    stats_ref[:, pl.ds(0, 128)] = jnp.where(
        part == 0, sum_aa, jnp.where(part == 1, sum_ab, jnp.where(part == 2, sum_bb, log_prop))
    )
    stats_ref[:, pl.ds(128, 128)] = log_fine


def split_three(value):
    high = value.astype(bf16)
    rest = value - high.astype(f32)
    middle = rest.astype(bf16)
    low = (rest - middle.astype(f32)).astype(bf16)
    return [high, middle, low]


def ray_kernel(stats_ref, ray_row_ref, rank_row_ref, live_ref, ray_col_ref, rank_col_ref, factor_ref, loss_ref, ahead):
    slots = stats_ref.shape[1]
    key_row = ray_row_ref[...] * 64 + rank_row_ref[...]
    rank_row = rank_row_ref[...]
    live = live_ref[...]
    sum_aa, sum_ab, sum_bb, log_prop, log_fine = (stats_ref[pl.ds(i, 1), :] for i in range(5))

    def stacked(values):
        pieces = [piece.astype(f32) for value in values for piece in split_three(value)]
        pieces += [jnp.zeros_like(pieces[0])] * (8 - len(pieces))
        return jnp.concatenate(pieces, axis=0).astype(bf16)

    logs = stacked([log_prop * live, log_fine * live])
    reached = jnp.zeros((8, slots), f32)
    for chunk in range(slots // 128):
        rows = pl.ds(chunk * 128, 128)
        gap = key_row - (ray_col_ref[rows, :] * 64 + rank_col_ref[rows, :])
        mask = jnp.where((gap > 0) & (gap <= rank_row), 1.0, 0.0).astype(bf16)
        ahead[rows, :] = mask
        reached = reached + jnp.dot(
            logs[:, chunk * 128 : (chunk + 1) * 128], mask, preferred_element_type=f32
        )
    entry_prop = jnp.exp(reached[0:1] + reached[1:2] + reached[2:3]) * live
    entry_fine = jnp.exp(reached[3:4] + reached[4:5] + reached[5:6]) * live
    seg_loss = (
        entry_prop * entry_prop * sum_aa
        - 2.0 * entry_prop * entry_fine * sum_ab
        + entry_fine * entry_fine * sum_bb
    )
    slot_grad = distill_weight * (entry_prop * sum_aa - entry_fine * sum_ab) * entry_prop
    carried = lax.dot_general(
        stacked([slot_grad]), ahead[...], LANES_BOTH, preferred_element_type=f32
    )
    factor_ref[pl.ds(0, 1), :] = 0.5 * distill_weight * entry_prop * entry_prop
    factor_ref[pl.ds(1, 1), :] = -distill_weight * entry_prop * entry_fine
    factor_ref[pl.ds(2, 1), :] = (carried[0:1] + carried[1:2] + carried[2:3]) * live
    factor_ref[pl.ds(3, 1), :] = jnp.zeros_like(live)
    losses = stacked([seg_loss])
    ray_loss = jnp.zeros((8, RAY_DEV), f32)
    ray_ids = lax.broadcasted_iota(jnp.int32, (128, RAY_DEV), 1)
    for chunk in range(slots // 128):
        mask = jnp.where(ray_col_ref[pl.ds(chunk * 128, 128), :] == ray_ids, 1.0, 0.0).astype(bf16)
        ray_loss = ray_loss + jnp.dot(
            losses[:, chunk * 128 : (chunk + 1) * 128], mask, preferred_element_type=f32
        )
    loss_ref[...] = 0.5 * distill_weight * (ray_loss[0:1] + ray_loss[1:2] + ray_loss[2:3])


def backward_kernel(factor_ref, back_ref, kept_ref, prop_out_ref, in_ref, out_ref, logit_grad, left):
    sources, rows_kept, width = kept_ref.shape
    rows_per = width // 128
    packed = factor_ref[...]
    part = lax.broadcasted_iota(jnp.int32, packed.shape, 1) // 32

    def to_samples(index):
        spread = group_total(jnp.where(part == index, packed, 0.0))
        return jnp.broadcast_to(spread[:, None, :], (sources, rows_per, 128)).reshape(
            sources * rows_per, 128
        )

    taken = back_ref[0]
    taken_grad = 2.0 * to_samples(0) * taken + to_samples(1) * back_ref[3]
    behind, unused = scan_segment(taken_grad * taken, rows_per, False)
    grad = (taken_grad * back_ref[1] - behind - to_samples(2)) * back_ref[2]
    logit_grad[...] = grad.astype(bf16).astype(f32)

    def accumulate(source, total):
        for part_index in range(rows_per):
            lanes = pl.ds(part_index * 128, 128)
            row = logit_grad[pl.ds(source * rows_per + part_index, 1), :]
            hidden = kept_ref[source, pl.ds(32, 16), lanes].astype(f32)
            wide = jnp.broadcast_to(row, (16, 128))
            left[pl.ds(0, 16), lanes] = jnp.where(hidden > 0, wide, 0.0).astype(bf16)
            left[pl.ds(16, 16), lanes] = wide.astype(bf16)
        return total + lax.dot_general(
            left[...], kept_ref[source], LANES_BOTH, preferred_element_type=f32
        )

    total = lax.fori_loop(0, sources, accumulate, jnp.zeros((32, rows_kept), f32))
    in_ref[...] = total[0:16, 0:32] * prop_out_ref[...]
    out_ref[...] = total[16:17, 32:48]


def vmem():
    return pl.BlockSpec(memory_space=pltpu.VMEM)


def on_device(
    feature_grid,
    fine_in,
    fine_mid,
    fine_out,
    prop_in,
    prop_out,
    sample_cells,
    sample_geometry,
    slot_ray,
    slot_rank,
    bucket_count,
):
    sources = lax.axis_size("dom")
    capacity = slot_ray.shape[3]
    width = sample_cells.shape[3]
    rows_all = sources * width // 128
    slots = sources * capacity
    cell_total = feature_grid.shape[2]
    params = pltpu.CompilerParams(vmem_limit_bytes=58 * 2**20)

    arrived = lax.all_to_all(sample_geometry, "dom", split_axis=3, concat_axis=3, tiled=True)
    kept, back, stats = pl.pallas_call(
        owner_kernel,
        out_shape=(
            jax.ShapeDtypeStruct((sources, 48, width), bf16),
            jax.ShapeDtypeStruct((4, rows_all, 128), f32),
            jax.ShapeDtypeStruct((sources, 256), f32),
        ),
        in_specs=[pl.BlockSpec(memory_space=pltpu.SMEM)] + [vmem()] * 7,
        out_specs=(vmem(), vmem(), vmem()),
        scratch_shapes=[
            pltpu.VMEM((cell_total, 128), f32),
            pltpu.VMEM((TILE, 128), f32),
            pltpu.VMEM((TILE, 128), f32),
            pltpu.VMEM((TILE, 128), f32),
            pltpu.VMEM((TILE, 128), f32),
            pltpu.VMEM((4, sources, width), f32),
            pltpu.VMEM((rows_all, 128), f32),
            pltpu.VMEM((rows_all, 128), f32),
            pltpu.VMEM((rows_all, 128), f32),
        ],
        compiler_params=params,
        name="owner_forward",
    )(
        sample_cells.reshape(sources, width),
        arrived.reshape(4, sources, width),
        feature_grid[0],
        fine_in[0],
        fine_mid[0],
        fine_out,
        prop_in[0],
        prop_out,
    )
    returned = lax.all_to_all(stats, "dom", split_axis=0, concat_axis=0, tiled=True)
    by_slot = (
        returned.reshape(sources, 8, capacity).transpose(1, 0, 2).reshape(8, slots)
    )
    live = (
        (jnp.arange(capacity)[None, :] < bucket_count[0, 0][:, None]).astype(f32).reshape(1, slots)
    )
    factors, ray_loss = pl.pallas_call(
        ray_kernel,
        out_shape=(
            jax.ShapeDtypeStruct((4, slots), f32),
            jax.ShapeDtypeStruct((1, RAY_DEV), f32),
        ),
        in_specs=[vmem()] * 6,
        out_specs=(vmem(), vmem()),
        scratch_shapes=[pltpu.VMEM((slots, slots), bf16)],
        compiler_params=params,
        name="ray_side",
    )(
        by_slot,
        slot_ray.reshape(1, slots),
        slot_rank.reshape(1, slots),
        live,
        slot_ray.reshape(slots, 1),
        slot_rank.reshape(slots, 1),
    )
    by_owner = factors.reshape(4, sources, capacity).transpose(1, 0, 2).reshape(sources, 4 * capacity)
    owner_factors = lax.all_to_all(by_owner, "dom", split_axis=0, concat_axis=0, tiled=True)
    in_grad, out_grad = pl.pallas_call(
        backward_kernel,
        out_shape=(
            jax.ShapeDtypeStruct((16, 32), f32),
            jax.ShapeDtypeStruct((1, 16), f32),
        ),
        in_specs=[vmem()] * 4,
        out_specs=(vmem(), vmem()),
        scratch_shapes=[pltpu.VMEM((rows_all, 128), f32), pltpu.VMEM((32, width), bf16)],
        compiler_params=params,
        name="owner_backward",
    )(owner_factors, back, kept, prop_out[0].astype(f32)[:, None])
    in_sum, out_sum = lax.psum((in_grad, out_grad), "rep")
    return (ray_loss.reshape(1, 1, -1), in_sum[None], out_sum)


def solution(mesh):
    return jax.shard_map(
        on_device,
        mesh=mesh,
        in_specs=(
            P("dom", None, None),
            P("dom", None, None),
            P("dom", None, None, None),
            P("dom", None),
            P("dom", None, None),
            P("dom", None),
            P("dom", "rep", None, None),
            P(None, "dom", "rep", None, None),
            P("dom", "rep", None, None),
            P("dom", "rep", None, None),
            P("dom", "rep", None),
        ),
        out_specs=(P("dom", "rep", None), P("dom", None, None), P("dom", None)),
        check_vma=False,
    )
```

```python
import functools

import jax
import jax.numpy as jnp
from jax import lax
from jax.experimental import pallas as pl
from jax.experimental.pallas import tpu as pltpu
from jax.sharding import PartitionSpec as P

GR = 32
RAY_DEV = 256
TILE = 1024
PART = 512

distill_weight = 50.0
f32 = jnp.float32
bf16 = jnp.bfloat16
LANES_BOTH = (((1,), (1,)), ((), ()))


def softplus(x):
    return jnp.maximum(x, 0.0) + jnp.log1p(jnp.exp(-jnp.abs(x)))


def group_total(x):
    once = x + pltpu.roll(x, 32, 1)
    return once + pltpu.roll(once, 64, 1)


def scan_segment(x, rows, forward):
    lane = lax.broadcasted_iota(jnp.int32, x.shape, 1)
    row = lax.broadcasted_iota(jnp.int32, x.shape, 0) % rows
    height = x.shape[0]

    def moved(value, step, axis):
        size = height if axis == 0 else 128
        return pltpu.roll(value, step if forward else size - step, axis)

    within = x
    for step in (32, 64):
        keep = lane >= step if forward else lane < 128 - step
        within = within + jnp.where(keep, moved(within, step, 1), 0.0)
    total = group_total(x)
    running = total
    step = 1
    while step < rows:
        keep = row >= step if forward else row < rows - step
        running = running + jnp.where(keep, moved(running, step, 0), 0.0)
        step *= 2
    edge = row >= 1 if forward else row < rows - 1
    return within + jnp.where(edge, moved(running, 1, 0), 0.0), total


def owner_kernel(
    cells_ref, geom_ref, grid_ref, fine_in_ref, fine_mid_ref, fine_out_ref, prop_in_ref, prop_out_ref,
    kept_ref, back_ref, stats_ref,
    table, even, odd, geo, fine_logit, prop_logit, spacing, even_cells, odd_cells, sems,
):
    sources, width = geom_ref.shape[1:]
    tiles_per = width // TILE
    tile_total = sources * tiles_per
    cell_blocks = grid_ref.shape[1] // 128
    rows_per = width // 128

    geo[...] = geom_ref[...].astype(f32)
    lane = lax.broadcasted_iota(jnp.int32, (GR, 128), 1)

    def build(second, block, carry):
        here = grid_ref[:, pl.ds(pl.multiple_of(block * 128, 128), 128)].astype(f32)
        after = jnp.minimum(block + 1, cell_blocks - 1)
        there = grid_ref[:, pl.ds(pl.multiple_of(after * 128, 128), 128)].astype(f32)
        pieces = [here]
        for shift in (1, GR, GR + 1):
            pieces.append(
                jnp.where(
                    lane < 128 - shift,
                    pltpu.roll(here, 128 - shift, 1),
                    pltpu.roll(there, 128 - shift, 1),
                )
            )
        turned = jnp.transpose(jnp.concatenate(pieces, axis=0))
        table[pl.ds(pl.multiple_of(block * 256, 256), 128, stride=2), :] = turned
        if second:
            earlier = pl.multiple_of((block - GR * GR // 128) * 256, 256)
            table[pl.ds(earlier + 1, 128, stride=2), :] = turned
        return carry

    slab = GR * GR // 128
    lax.fori_loop(0, slab, functools.partial(build, False), 0)
    lax.fori_loop(slab, cell_blocks, functools.partial(build, True), 0, unroll=2)

    first = jnp.concatenate([fine_in_ref[...], prop_in_ref[...]], axis=0)
    hidden = fine_in_ref.shape[0]
    eye = (
        lax.broadcasted_iota(jnp.int32, (256, 256), 0)
        == lax.broadcasted_iota(jnp.int32, (256, 256), 1)
    ).astype(f32).astype(bf16)

    def fetch(tile, indices, sem):
        start = pl.multiple_of(jnp.minimum(tile, tile_total - 1) * TILE, TILE)
        return pltpu.make_async_copy(cells_ref.at[pl.ds(start, TILE)], indices, sem)

    def gather(indices, low, start=0, stop=TILE):
        for j in range(start, stop):
            cell = pl.multiple_of(indices[j], 2)
            low[pl.ds(2 * j, 2), :] = table[pl.ds(cell, 2), :]

    def evaluate(tile, low, part):
        source = tile // tiles_per
        first_lane = (tile % tiles_per) * TILE
        if True:
            lanes = pl.ds(pl.multiple_of(first_lane + part * PART, PART), PART)
            start = 2 * part * PART
            rows = jnp.concatenate(
                [
                    low[pl.ds(start, PART, stride=2), :],
                    low[pl.ds(start + 1, PART, stride=2), :],
                ],
                axis=1,
            ).astype(bf16)
            turned = lax.dot_general(eye, rows, LANES_BOTH, preferred_element_type=f32)
            yield
            offsets = [geo[axis, pl.ds(source, 1), lanes] for axis in range(3)]
            factors = [[1.0 - value, value] for value in offsets]
            summed = jnp.zeros((32, PART), f32)
            for corner in range(8):
                factor = (
                    factors[0][corner // 4]
                    * factors[1][corner // 2 % 2]
                    * factors[2][corner % 2]
                )
                summed = summed + turned[corner * 32 : (corner + 1) * 32] * factor
            features = summed.astype(bf16)
            kept_ref[source, pl.ds(0, 32), lanes] = features
            yield
            both = jnp.maximum(
                jnp.dot(first, features, preferred_element_type=f32), 0.0
            ).astype(bf16)
            prop_hidden = both[hidden:]
            fine_hidden = both[:hidden]
            kept_ref[source, pl.ds(32, 16), lanes] = prop_hidden
            yield
            for layer in range(fine_mid_ref.shape[0]):
                fine_hidden = jnp.maximum(
                    jnp.dot(fine_mid_ref[layer], fine_hidden, preferred_element_type=f32), 0.0
                ).astype(bf16)
                yield
            fine = jnp.dot(fine_out_ref[...], fine_hidden, preferred_element_type=f32)
            prop = jnp.dot(prop_out_ref[...], prop_hidden, preferred_element_type=f32)
            gap = geo[3, pl.ds(source, 1), lanes]
            for piece in range(PART // 128):
                row = pl.ds(tile * (TILE // 128) + (part * PART) // 128 + piece, 1)
                cut = slice(piece * 128, (piece + 1) * 128)
                fine_logit[row, :] = fine[:, cut]
                prop_logit[row, :] = prop[:, cut]
                spacing[row, :] = gap[:, cut]
            yield

    def weave(indices, into, tile, out_of):
        parts = TILE // PART
        stages = 4 + fine_mid_ref.shape[0]
        slots = stages + parts - 1
        running = [evaluate(tile, out_of, part) for part in range(parts)]
        for slot in range(slots):
            for part in range(parts):
                if 0 <= slot - part < stages:
                    next(running[part])
            gather(indices, into, slot * TILE // slots, (slot + 1) * TILE // slots)

    fetch(0, even_cells, sems.at[0]).start()
    fetch(1, odd_cells, sems.at[1]).start()
    fetch(0, even_cells, sems.at[0]).wait()
    gather(even_cells, even)

    def step(tile, carry):
        @pl.when(tile % 2 == 0)
        def _():
            fetch(tile + 2, even_cells, sems.at[0]).start()
            fetch(tile + 1, odd_cells, sems.at[1]).wait()
            weave(odd_cells, odd, tile, even)

        @pl.when(tile % 2 == 1)
        def _():
            fetch(tile + 2, odd_cells, sems.at[1]).start()
            fetch(tile + 1, even_cells, sems.at[0]).wait()
            weave(even_cells, even, tile, odd)

        return carry

    lax.fori_loop(0, tile_total, step, 0)
    fetch(tile_total, odd_cells, sems.at[1]).wait()

    gap = spacing[...]
    prop_raw = prop_logit[...]
    optical = softplus(prop_raw) * gap
    depth, prop_total = scan_segment(optical, rows_per, True)
    before = jnp.exp(optical - depth)
    prop_taken = before - jnp.exp(-depth)
    back_ref[0] = prop_taken
    back_ref[1] = before
    back_ref[2] = gap * jax.nn.sigmoid(prop_raw)
    fine_optical = softplus(fine_logit[...]) * gap
    fine_depth, fine_total = scan_segment(fine_optical, rows_per, True)
    fine_taken = jnp.exp(fine_optical - fine_depth) - jnp.exp(-fine_depth)
    back_ref[3] = fine_taken

    def per_segment(value, totalled):
        over_rows = jnp.sum(value.reshape(sources, rows_per, 128), axis=1)
        return over_rows if totalled else group_total(over_rows)

    sum_aa = per_segment(prop_taken * prop_taken, False)
    sum_ab = per_segment(prop_taken * fine_taken, False)
    sum_bb = per_segment(fine_taken * fine_taken, False)
    log_prop = -per_segment(prop_total, True)
    log_fine = -per_segment(fine_total, True)
    part = lax.broadcasted_iota(jnp.int32, (sources, 128), 1) // 32
    stats_ref[:, pl.ds(0, 128)] = jnp.where(
        part == 0, sum_aa, jnp.where(part == 1, sum_ab, jnp.where(part == 2, sum_bb, log_prop))
    )
    stats_ref[:, pl.ds(128, 128)] = log_fine


def split_three(value):
    high = value.astype(bf16)
    rest = value - high.astype(f32)
    middle = rest.astype(bf16)
    low = (rest - middle.astype(f32)).astype(bf16)
    return [high, middle, low]


def ray_kernel(stats_ref, ray_row_ref, rank_row_ref, live_ref, ray_col_ref, rank_col_ref, factor_ref, loss_ref, ahead):
    slots = stats_ref.shape[1]
    key_row = ray_row_ref[...] * 64 + rank_row_ref[...]
    rank_row = rank_row_ref[...]
    live = live_ref[...]
    sum_aa, sum_ab, sum_bb, log_prop, log_fine = (stats_ref[pl.ds(i, 1), :] for i in range(5))

    def stacked(values):
        pieces = [piece.astype(f32) for value in values for piece in split_three(value)]
        pieces += [jnp.zeros_like(pieces[0])] * (8 - len(pieces))
        return jnp.concatenate(pieces, axis=0).astype(bf16)

    logs = stacked([log_prop * live, log_fine * live])
    reached = jnp.zeros((8, slots), f32)
    for chunk in range(slots // 128):
        rows = pl.ds(chunk * 128, 128)
        gap = key_row - (ray_col_ref[rows, :] * 64 + rank_col_ref[rows, :])
        mask = jnp.where((gap > 0) & (gap <= rank_row), 1.0, 0.0).astype(bf16)
        ahead[rows, :] = mask
        reached = reached + jnp.dot(
            logs[:, chunk * 128 : (chunk + 1) * 128], mask, preferred_element_type=f32
        )
    entry_prop = jnp.exp(reached[0:1] + reached[1:2] + reached[2:3]) * live
    entry_fine = jnp.exp(reached[3:4] + reached[4:5] + reached[5:6]) * live
    seg_loss = (
        entry_prop * entry_prop * sum_aa
        - 2.0 * entry_prop * entry_fine * sum_ab
        + entry_fine * entry_fine * sum_bb
    )
    slot_grad = distill_weight * (entry_prop * sum_aa - entry_fine * sum_ab) * entry_prop
    carried = lax.dot_general(
        stacked([slot_grad]), ahead[...], LANES_BOTH, preferred_element_type=f32
    )
    factor_ref[pl.ds(0, 1), :] = 0.5 * distill_weight * entry_prop * entry_prop
    factor_ref[pl.ds(1, 1), :] = -distill_weight * entry_prop * entry_fine
    factor_ref[pl.ds(2, 1), :] = (carried[0:1] + carried[1:2] + carried[2:3]) * live
    factor_ref[pl.ds(3, 1), :] = jnp.zeros_like(live)
    losses = stacked([seg_loss])
    ray_loss = jnp.zeros((8, RAY_DEV), f32)
    ray_ids = lax.broadcasted_iota(jnp.int32, (128, RAY_DEV), 1)
    for chunk in range(slots // 128):
        mask = jnp.where(ray_col_ref[pl.ds(chunk * 128, 128), :] == ray_ids, 1.0, 0.0).astype(bf16)
        ray_loss = ray_loss + jnp.dot(
            losses[:, chunk * 128 : (chunk + 1) * 128], mask, preferred_element_type=f32
        )
    loss_ref[...] = 0.5 * distill_weight * (ray_loss[0:1] + ray_loss[1:2] + ray_loss[2:3])


def backward_kernel(factor_ref, back_ref, kept_ref, prop_out_ref, in_ref, out_ref, logit_grad, left):
    sources, rows_kept, width = kept_ref.shape
    rows_per = width // 128
    packed = factor_ref[...]
    part = lax.broadcasted_iota(jnp.int32, packed.shape, 1) // 32

    def to_samples(index):
        spread = group_total(jnp.where(part == index, packed, 0.0))
        return jnp.broadcast_to(spread[:, None, :], (sources, rows_per, 128)).reshape(
            sources * rows_per, 128
        )

    taken = back_ref[0]
    taken_grad = 2.0 * to_samples(0) * taken + to_samples(1) * back_ref[3]
    behind, unused = scan_segment(taken_grad * taken, rows_per, False)
    grad = (taken_grad * back_ref[1] - behind - to_samples(2)) * back_ref[2]
    logit_grad[...] = grad.astype(bf16).astype(f32)

    def accumulate(source, total):
        for part_index in range(rows_per):
            lanes = pl.ds(part_index * 128, 128)
            row = logit_grad[pl.ds(source * rows_per + part_index, 1), :]
            hidden = kept_ref[source, pl.ds(32, 16), lanes].astype(f32)
            wide = jnp.broadcast_to(row, (16, 128))
            left[pl.ds(0, 16), lanes] = jnp.where(hidden > 0, wide, 0.0).astype(bf16)
            left[pl.ds(16, 16), lanes] = wide.astype(bf16)
        return total + lax.dot_general(
            left[...], kept_ref[source], LANES_BOTH, preferred_element_type=f32
        )

    total = lax.fori_loop(0, sources, accumulate, jnp.zeros((32, rows_kept), f32))
    in_ref[...] = total[0:16, 0:32] * prop_out_ref[...]
    out_ref[...] = total[16:17, 32:48]


def vmem():
    return pl.BlockSpec(memory_space=pltpu.VMEM)


def on_device(
    feature_grid,
    fine_in,
    fine_mid,
    fine_out,
    prop_in,
    prop_out,
    sample_cells,
    sample_geometry,
    slot_ray,
    slot_rank,
    bucket_count,
):
    sources = lax.axis_size("dom")
    capacity = slot_ray.shape[3]
    width = sample_cells.shape[3]
    rows_all = sources * width // 128
    slots = sources * capacity
    cell_total = feature_grid.shape[2]
    params = pltpu.CompilerParams(vmem_limit_bytes=58 * 2**20)

    arrived = lax.all_to_all(sample_geometry, "dom", split_axis=3, concat_axis=3, tiled=True)
    kept, back, stats = pl.pallas_call(
        owner_kernel,
        out_shape=(
            jax.ShapeDtypeStruct((sources, 48, width), bf16),
            jax.ShapeDtypeStruct((4, rows_all, 128), f32),
            jax.ShapeDtypeStruct((sources, 256), f32),
        ),
        in_specs=[pl.BlockSpec(memory_space=pl.ANY)] + [vmem()] * 7,
        out_specs=(vmem(), vmem(), vmem()),
        scratch_shapes=[
            pltpu.VMEM((2 * cell_total, 128), f32),
            pltpu.VMEM((2 * TILE, 128), f32),
            pltpu.VMEM((2 * TILE, 128), f32),
            pltpu.VMEM((4, sources, width), f32),
            pltpu.VMEM((rows_all, 128), f32),
            pltpu.VMEM((rows_all, 128), f32),
            pltpu.VMEM((rows_all, 128), f32),
            pltpu.SMEM((TILE,), jnp.int32),
            pltpu.SMEM((TILE,), jnp.int32),
            pltpu.SemaphoreType.DMA((2,)),
        ],
        compiler_params=params,
        name="owner_forward",
    )(
        (sample_cells * 2).reshape(sources * width),
        arrived.reshape(4, sources, width),
        feature_grid[0],
        fine_in[0],
        fine_mid[0],
        fine_out,
        prop_in[0],
        prop_out,
    )
    returned = lax.all_to_all(stats, "dom", split_axis=0, concat_axis=0, tiled=True)
    by_slot = (
        returned.reshape(sources, 8, capacity).transpose(1, 0, 2).reshape(8, slots)
    )
    live = (
        (jnp.arange(capacity)[None, :] < bucket_count[0, 0][:, None]).astype(f32).reshape(1, slots)
    )
    factors, ray_loss = pl.pallas_call(
        ray_kernel,
        out_shape=(
            jax.ShapeDtypeStruct((4, slots), f32),
            jax.ShapeDtypeStruct((1, RAY_DEV), f32),
        ),
        in_specs=[vmem()] * 6,
        out_specs=(vmem(), vmem()),
        scratch_shapes=[pltpu.VMEM((slots, slots), bf16)],
        compiler_params=params,
        name="ray_side",
    )(
        by_slot,
        slot_ray.reshape(1, slots),
        slot_rank.reshape(1, slots),
        live,
        slot_ray.reshape(slots, 1),
        slot_rank.reshape(slots, 1),
    )
    by_owner = factors.reshape(4, sources, capacity).transpose(1, 0, 2).reshape(sources, 4 * capacity)
    owner_factors = lax.all_to_all(by_owner, "dom", split_axis=0, concat_axis=0, tiled=True)
    in_grad, out_grad = pl.pallas_call(
        backward_kernel,
        out_shape=(
            jax.ShapeDtypeStruct((16, 32), f32),
            jax.ShapeDtypeStruct((1, 16), f32),
        ),
        in_specs=[vmem()] * 4,
        out_specs=(vmem(), vmem()),
        scratch_shapes=[pltpu.VMEM((rows_all, 128), f32), pltpu.VMEM((32, width), bf16)],
        compiler_params=params,
        name="owner_backward",
    )(owner_factors, back, kept, prop_out[0].astype(f32)[:, None])
    in_sum, out_sum = lax.psum((in_grad, out_grad), "rep")
    return (ray_loss.reshape(1, 1, -1), in_sum[None], out_sum)


def solution(mesh):
    return jax.shard_map(
        on_device,
        mesh=mesh,
        in_specs=(
            P("dom", None, None),
            P("dom", None, None),
            P("dom", None, None, None),
            P("dom", None),
            P("dom", None, None),
            P("dom", None),
            P("dom", "rep", None, None),
            P(None, "dom", "rep", None, None),
            P("dom", "rep", None, None),
            P("dom", "rep", None, None),
            P("dom", "rep", None),
        ),
        out_specs=(P("dom", "rep", None), P("dom", None, None), P("dom", None)),
        check_vma=False,
    )
```

```python
import functools

import jax
import jax.numpy as jnp
from jax import lax
from jax.experimental import pallas as pl
from jax.experimental.pallas import tpu as pltpu
from jax.sharding import PartitionSpec as P

GR = 32
RAY_DEV = 256
TILE = 1024
PART = 512

distill_weight = 50.0
f32 = jnp.float32
bf16 = jnp.bfloat16
LANES_BOTH = (((1,), (1,)), ((), ()))
MESH = pl.DeviceIdType.MESH


def softplus(x):
    return jnp.maximum(x, 0.0) + jnp.log1p(jnp.exp(-jnp.abs(x)))


def group_total(x):
    once = x + pltpu.roll(x, 32, 1)
    return once + pltpu.roll(once, 64, 1)


def scan_segment(x, rows, forward):
    lane = lax.broadcasted_iota(jnp.int32, x.shape, 1)
    row = lax.broadcasted_iota(jnp.int32, x.shape, 0) % rows
    height = x.shape[0]

    def moved(value, step, axis):
        size = height if axis == 0 else 128
        return pltpu.roll(value, step if forward else size - step, axis)

    within = x
    for step in (32, 64):
        keep = lane >= step if forward else lane < 128 - step
        within = within + jnp.where(keep, moved(within, step, 1), 0.0)
    total = group_total(x)
    running = total
    step = 1
    while step < rows:
        keep = row >= step if forward else row < rows - step
        running = running + jnp.where(keep, moved(running, step, 0), 0.0)
        step *= 2
    edge = row >= 1 if forward else row < rows - 1
    return within + jnp.where(edge, moved(running, 1, 0), 0.0), total


def owner_kernel(
    cells_ref, geom_ref, grid_ref, fine_in_ref, fine_mid_ref, fine_out_ref, prop_in_ref, prop_out_ref,
    kept_ref, back_ref, stats_ref,
    table, even, odd, geo, fine_logit, prop_logit, spacing, even_cells, odd_cells, sems,
):
    sources, width = geom_ref.shape[1:]
    tiles_per = width // TILE
    tile_total = sources * tiles_per
    cell_blocks = grid_ref.shape[1] // 128
    rows_per = width // 128

    geo[...] = geom_ref[...].astype(f32)
    lane = lax.broadcasted_iota(jnp.int32, (GR, 128), 1)

    def build(second, block, carry):
        here = grid_ref[:, pl.ds(pl.multiple_of(block * 128, 128), 128)].astype(f32)
        after = jnp.minimum(block + 1, cell_blocks - 1)
        there = grid_ref[:, pl.ds(pl.multiple_of(after * 128, 128), 128)].astype(f32)
        pieces = [here]
        for shift in (1, GR, GR + 1):
            pieces.append(
                jnp.where(
                    lane < 128 - shift,
                    pltpu.roll(here, 128 - shift, 1),
                    pltpu.roll(there, 128 - shift, 1),
                )
            )
        turned = jnp.transpose(jnp.concatenate(pieces, axis=0))
        table[pl.ds(pl.multiple_of(block * 256, 256), 128, stride=2), :] = turned
        if second:
            earlier = pl.multiple_of((block - GR * GR // 128) * 256, 256)
            table[pl.ds(earlier + 1, 128, stride=2), :] = turned
        return carry

    slab = GR * GR // 128
    lax.fori_loop(0, slab, functools.partial(build, False), 0)
    lax.fori_loop(slab, cell_blocks, functools.partial(build, True), 0, unroll=2)

    first = jnp.concatenate([fine_in_ref[...], prop_in_ref[...]], axis=0)
    hidden = fine_in_ref.shape[0]
    eye = (
        lax.broadcasted_iota(jnp.int32, (256, 256), 0)
        == lax.broadcasted_iota(jnp.int32, (256, 256), 1)
    ).astype(f32).astype(bf16)

    def fetch(tile, indices, sem):
        start = pl.multiple_of(jnp.minimum(tile, tile_total - 1) * TILE, TILE)
        return pltpu.make_async_copy(cells_ref.at[pl.ds(start, TILE)], indices, sem)

    def gather(indices, low, start=0, stop=TILE):
        for j in range(start, stop):
            cell = pl.multiple_of(indices[j], 2)
            low[pl.ds(2 * j, 2), :] = table[pl.ds(cell, 2), :]

    def evaluate(tile, low, part):
        source = tile // tiles_per
        first_lane = (tile % tiles_per) * TILE
        if True:
            lanes = pl.ds(pl.multiple_of(first_lane + part * PART, PART), PART)
            start = 2 * part * PART
            rows = jnp.concatenate(
                [
                    low[pl.ds(start, PART, stride=2), :],
                    low[pl.ds(start + 1, PART, stride=2), :],
                ],
                axis=1,
            ).astype(bf16)
            turned = lax.dot_general(eye, rows, LANES_BOTH, preferred_element_type=f32)
            yield
            offsets = [geo[axis, pl.ds(source, 1), lanes] for axis in range(3)]
            factors = [[1.0 - value, value] for value in offsets]
            summed = jnp.zeros((32, PART), f32)
            for corner in range(8):
                factor = (
                    factors[0][corner // 4]
                    * factors[1][corner // 2 % 2]
                    * factors[2][corner % 2]
                )
                summed = summed + turned[corner * 32 : (corner + 1) * 32] * factor
            features = summed.astype(bf16)
            kept_ref[source, pl.ds(0, 32), lanes] = features
            yield
            both = jnp.maximum(
                jnp.dot(first, features, preferred_element_type=f32), 0.0
            ).astype(bf16)
            prop_hidden = both[hidden:]
            fine_hidden = both[:hidden]
            kept_ref[source, pl.ds(32, 16), lanes] = prop_hidden
            yield
            for layer in range(fine_mid_ref.shape[0]):
                fine_hidden = jnp.maximum(
                    jnp.dot(fine_mid_ref[layer], fine_hidden, preferred_element_type=f32), 0.0
                ).astype(bf16)
                yield
            fine = jnp.dot(fine_out_ref[...], fine_hidden, preferred_element_type=f32)
            prop = jnp.dot(prop_out_ref[...], prop_hidden, preferred_element_type=f32)
            gap = geo[3, pl.ds(source, 1), lanes]
            for piece in range(PART // 128):
                row = pl.ds(tile * (TILE // 128) + (part * PART) // 128 + piece, 1)
                cut = slice(piece * 128, (piece + 1) * 128)
                fine_logit[row, :] = fine[:, cut]
                prop_logit[row, :] = prop[:, cut]
                spacing[row, :] = gap[:, cut]
            yield

    def weave(indices, into, tile, out_of):
        parts = TILE // PART
        stages = 4 + fine_mid_ref.shape[0]
        slots = stages + parts - 1
        running = [evaluate(tile, out_of, part) for part in range(parts)]
        for slot in range(slots):
            for part in range(parts):
                if 0 <= slot - part < stages:
                    next(running[part])
            gather(indices, into, slot * TILE // slots, (slot + 1) * TILE // slots)

    fetch(0, even_cells, sems.at[0]).start()
    fetch(1, odd_cells, sems.at[1]).start()
    fetch(0, even_cells, sems.at[0]).wait()
    gather(even_cells, even)

    def step(tile, carry):
        @pl.when(tile % 2 == 0)
        def _():
            fetch(tile + 2, even_cells, sems.at[0]).start()
            fetch(tile + 1, odd_cells, sems.at[1]).wait()
            weave(odd_cells, odd, tile, even)

        @pl.when(tile % 2 == 1)
        def _():
            fetch(tile + 2, odd_cells, sems.at[1]).start()
            fetch(tile + 1, even_cells, sems.at[0]).wait()
            weave(even_cells, even, tile, odd)

        return carry

    lax.fori_loop(0, tile_total, step, 0)
    fetch(tile_total, odd_cells, sems.at[1]).wait()

    gap = spacing[...]
    prop_raw = prop_logit[...]
    optical = softplus(prop_raw) * gap
    depth, prop_total = scan_segment(optical, rows_per, True)
    before = jnp.exp(optical - depth)
    prop_taken = before - jnp.exp(-depth)
    back_ref[0] = prop_taken
    back_ref[1] = before
    back_ref[2] = gap * jax.nn.sigmoid(prop_raw)
    fine_optical = softplus(fine_logit[...]) * gap
    fine_depth, fine_total = scan_segment(fine_optical, rows_per, True)
    fine_taken = jnp.exp(fine_optical - fine_depth) - jnp.exp(-fine_depth)
    back_ref[3] = fine_taken

    def per_segment(value, totalled):
        over_rows = jnp.sum(value.reshape(sources, rows_per, 128), axis=1)
        return over_rows if totalled else group_total(over_rows)

    sum_aa = per_segment(prop_taken * prop_taken, False)
    sum_ab = per_segment(prop_taken * fine_taken, False)
    sum_bb = per_segment(fine_taken * fine_taken, False)
    log_prop = -per_segment(prop_total, True)
    log_fine = -per_segment(fine_total, True)
    part = lax.broadcasted_iota(jnp.int32, (sources, 128), 1) // 32
    stats_ref[:, 0, :] = jnp.where(
        part == 0, sum_aa, jnp.where(part == 1, sum_ab, jnp.where(part == 2, sum_bb, log_prop))
    )
    stats_ref[:, 1, :] = log_fine


def split_three(value):
    high = value.astype(bf16)
    rest = value - high.astype(f32)
    middle = rest.astype(bf16)
    low = (rest - middle.astype(f32)).astype(bf16)
    return [high, middle, low]


def finish_kernel(
    stats_ref, ray_ref, rank_ref, count_ref, prop_out_ref, back_hbm, kept_hbm,
    loss_ref, in_ref, out_ref,
    stats_in, factors_out, factors_in, grads_in, flat, ahead, logit_grad, left, back_ref, kept_ref,
    stats_send, stats_recv, factors_send, factors_recv, grads_send, grads_recv, local,
):
    sources, rows_kept, width = kept_ref.shape
    rows_per = width // 128
    slots = ahead.shape[0]
    blocks = slots // 128
    me, replica = lax.axis_index("dom"), lax.axis_index("rep")
    replicas = lax.axis_size("rep")

    load_kept = pltpu.make_async_copy(kept_hbm, kept_ref, local.at[0])
    load_back = pltpu.make_async_copy(back_hbm, back_ref, local.at[1])
    load_back.start()
    load_kept.start()

    barrier = pltpu.get_barrier_semaphore()

    def greet(step, carry):
        peer = lax.rem(me + step, sources)
        pl.semaphore_signal(barrier, inc=1, device_id=(peer, replica), device_id_type=MESH)
        return carry

    lax.fori_loop(1, sources, greet, 0)
    for step in range(1, replicas):
        other = lax.rem(replica + step, replicas)
        pl.semaphore_signal(barrier, inc=1, device_id=(me, other), device_id_type=MESH)
    pl.semaphore_wait(barrier, sources + replicas - 2)

    def exchange(source, target, send, recv):
        def copy(step):
            peer = lax.rem(me + step, sources)
            return pltpu.make_async_remote_copy(
                src_ref=source.at[peer],
                dst_ref=target.at[me],
                send_sem=send.at[step],
                recv_sem=recv.at[step],
                device_id=(peer, replica),
                device_id_type=MESH,
            )

        def start(step, carry):
            copy(step).start()
            return carry

        def finish(step, carry):
            copy(step).wait()
            return carry

        lax.fori_loop(1, sources, start, 0)
        return lambda: lax.fori_loop(1, sources, finish, 0)

    wait_stats = exchange(stats_ref, stats_in, stats_send, stats_recv)
    own_stats = pltpu.make_async_copy(stats_ref.at[me], stats_in.at[me], local.at[2])
    own_stats.start()

    part_row = lax.broadcasted_iota(jnp.int32, (sources, 128), 0)
    group = lax.broadcasted_iota(jnp.int32, (sources, 128), 1) // 32
    seat = part_row % 4
    fold = jnp.where(
        lax.broadcasted_iota(jnp.int32, (blocks, sources), 0)
        == lax.broadcasted_iota(jnp.int32, (blocks, sources), 1) // 4,
        1.0,
        0.0,
    )
    unfold = jnp.where(
        lax.broadcasted_iota(jnp.int32, (sources, blocks), 0) // 4
        == lax.broadcasted_iota(jnp.int32, (sources, blocks), 1),
        1.0,
        0.0,
    )

    def exact(first, second):
        return jnp.dot(first, second, precision=lax.Precision.HIGHEST, preferred_element_type=f32)

    def dense(seated):
        return exact(fold, jnp.where(group == seat, seated, 0.0))

    def four(value):
        return jnp.concatenate([value] * 4, axis=1)

    def as_row(value):
        return jnp.concatenate([value[b : b + 1] for b in range(blocks)], axis=1)

    def as_dense(value):
        return jnp.concatenate(
            [value[:, b * 128 : (b + 1) * 128] for b in range(blocks)], axis=0
        )

    counts = jnp.broadcast_to(count_ref[...].astype(f32), (sources, sources))
    diagonal = lax.broadcasted_iota(jnp.int32, (sources, sources), 0) == lax.broadcasted_iota(
        jnp.int32, (sources, sources), 1
    )
    count_column = jnp.sum(jnp.where(diagonal, counts, 0.0), axis=1, keepdims=True)
    slot_lane = (lax.broadcasted_iota(jnp.int32, (sources, 128), 1) % 32).astype(f32)
    live = as_row(dense(jnp.where(slot_lane < count_column, 1.0, 0.0)))
    rays = dense(four(ray_ref[...].astype(f32)))
    ranks = dense(four(rank_ref[...].astype(f32)))
    keys = rays * 64.0 + ranks
    key_row, rank_row = as_row(keys), as_row(ranks)
    key_column, ray_column = jnp.transpose(keys), jnp.transpose(rays)
    for chunk in range(blocks):
        gap = key_row - key_column[:, chunk : chunk + 1]
        ahead[pl.ds(chunk * 128, 128), :] = jnp.where(
            (gap > 0.5) & (gap < rank_row + 0.5), 1.0, 0.0
        ).astype(bf16)

    own_stats.wait()
    wait_stats()

    for index in range(sources):
        flat[pl.ds(index, 1), :] = stats_in[index, pl.ds(0, 1), :]
    packed = flat[...]
    turned = [packed] + [pltpu.roll(packed, 32 * step, 1) for step in range(1, 4)]

    def stat(index):
        value = turned[(3 - index) % 4]
        for place in range(3):
            value = jnp.where(seat == place, turned[(place - index) % 4], value)
        return as_row(dense(value))

    sum_aa, sum_ab, sum_bb, log_prop = (stat(index) for index in range(4))
    for index in range(sources):
        flat[pl.ds(index, 1), :] = stats_in[index, pl.ds(1, 1), :]
    log_fine = as_row(dense(flat[...]))

    def stacked(values):
        pieces = [piece.astype(f32) for value in values for piece in split_three(value)]
        pieces += [jnp.zeros_like(pieces[0])] * (8 - len(pieces))
        return jnp.concatenate(pieces, axis=0).astype(bf16)

    logs = stacked([log_prop * live, log_fine * live])
    reached = jnp.dot(logs, ahead[...], preferred_element_type=f32)
    entry_prop = jnp.exp(reached[0:1] + reached[1:2] + reached[2:3]) * live
    entry_fine = jnp.exp(reached[3:4] + reached[4:5] + reached[5:6]) * live
    slot_grad = distill_weight * (entry_prop * sum_aa - entry_fine * sum_ab) * entry_prop
    carried = lax.dot_general(
        stacked([slot_grad]), ahead[...], LANES_BOTH, preferred_element_type=f32
    )
    outgoing = (
        0.5 * distill_weight * entry_prop * entry_prop,
        -distill_weight * entry_prop * entry_fine,
        (carried[0:1] + carried[1:2] + carried[2:3]) * live,
    )
    message = jnp.zeros((sources, 128), f32)
    for index, value in enumerate(outgoing):
        spread = exact(unfold, as_dense(value))
        for place in range(4):
            shift = 32 * ((index - place) % 4)
            moved = pltpu.roll(spread, shift, 1) if shift else spread
            message = jnp.where((group == index) & (seat == place), moved, message)
    for index in range(sources):
        factors_out[index] = message[index : index + 1]

    wait_factors = exchange(factors_out, factors_in, factors_send, factors_recv)
    own_factors = pltpu.make_async_copy(factors_out.at[me], factors_in.at[me], local.at[3])
    own_factors.start()

    seg_loss = (
        entry_prop * entry_prop * sum_aa
        - 2.0 * entry_prop * entry_fine * sum_ab
        + entry_fine * entry_fine * sum_bb
    )
    losses = stacked([seg_loss])
    ray_loss = jnp.zeros((8, RAY_DEV), f32)
    ray_ids = lax.broadcasted_iota(jnp.int32, (128, RAY_DEV), 1).astype(f32)
    for chunk in range(blocks):
        mask = jnp.where(ray_column[:, chunk : chunk + 1] == ray_ids, 1.0, 0.0).astype(bf16)
        ray_loss = ray_loss + jnp.dot(
            losses[:, chunk * 128 : (chunk + 1) * 128], mask, preferred_element_type=f32
        )
    loss_ref[...] = 0.5 * distill_weight * (ray_loss[0:1] + ray_loss[1:2] + ray_loss[2:3])

    load_back.wait()
    load_kept.wait()
    own_factors.wait()
    wait_factors()

    for index in range(sources):
        flat[pl.ds(index, 1), :] = factors_in[index]
    factors = flat[...]

    def to_samples(index):
        spread = group_total(jnp.where(group == index, factors, 0.0))
        return jnp.broadcast_to(spread[:, None, :], (sources, rows_per, 128)).reshape(
            sources * rows_per, 128
        )

    taken = back_ref[0]
    taken_grad = 2.0 * to_samples(0) * taken + to_samples(1) * back_ref[3]
    behind, unused = scan_segment(taken_grad * taken, rows_per, False)
    grad = (taken_grad * back_ref[1] - behind - to_samples(2)) * back_ref[2]
    logit_grad[...] = grad.astype(bf16).astype(f32)

    def accumulate(source, total):
        for part_index in range(rows_per):
            lanes = pl.ds(part_index * 128, 128)
            row = logit_grad[pl.ds(source * rows_per + part_index, 1), :]
            hidden = kept_ref[source, pl.ds(32, 16), lanes].astype(f32)
            wide = jnp.broadcast_to(row, (16, 128))
            left[pl.ds(0, 16), lanes] = jnp.where(hidden > 0, wide, 0.0).astype(bf16)
            left[pl.ds(16, 16), lanes] = wide.astype(bf16)
        return total + lax.dot_general(
            left[...], kept_ref[source], LANES_BOTH, preferred_element_type=f32
        )

    total = lax.fori_loop(0, sources, accumulate, jnp.zeros((32, rows_kept), f32))
    grads_in[replica] = jnp.concatenate([total, jnp.zeros((32, 128 - rows_kept), f32)], axis=1)

    def share(step):
        other = lax.rem(replica + step, replicas)
        return pltpu.make_async_remote_copy(
            src_ref=grads_in.at[replica],
            dst_ref=grads_in.at[replica],
            send_sem=grads_send.at[step],
            recv_sem=grads_recv.at[step],
            device_id=(me, other),
            device_id_type=MESH,
        )

    for step in range(1, replicas):
        share(step).start()
    for step in range(1, replicas):
        share(step).wait()
    summed = grads_in[0]
    for index in range(1, replicas):
        summed = summed + grads_in[index]
    in_ref[...] = summed[0:16, 0:32] * prop_out_ref[...]
    out_ref[...] = summed[16:17, 32:48]


def vmem():
    return pl.BlockSpec(memory_space=pltpu.VMEM)


def on_device(
    feature_grid,
    fine_in,
    fine_mid,
    fine_out,
    prop_in,
    prop_out,
    sample_cells,
    sample_geometry,
    slot_ray,
    slot_rank,
    bucket_count,
):
    sources = lax.axis_size("dom")
    capacity = slot_ray.shape[3]
    width = sample_cells.shape[3]
    rows_all = sources * width // 128
    slots = sources * capacity
    cell_total = feature_grid.shape[2]
    params = pltpu.CompilerParams(vmem_limit_bytes=58 * 2**20)

    arrived = lax.all_to_all(sample_geometry, "dom", split_axis=3, concat_axis=3, tiled=True)
    kept, back, stats = pl.pallas_call(
        owner_kernel,
        out_shape=(
            jax.ShapeDtypeStruct((sources, 48, width), bf16),
            jax.ShapeDtypeStruct((4, rows_all, 128), f32),
            jax.ShapeDtypeStruct((sources, 2, 128), f32),
        ),
        in_specs=[pl.BlockSpec(memory_space=pl.ANY)] + [vmem()] * 7,
        out_specs=(vmem(), vmem(), vmem()),
        scratch_shapes=[
            pltpu.VMEM((2 * cell_total, 128), f32),
            pltpu.VMEM((2 * TILE, 128), f32),
            pltpu.VMEM((2 * TILE, 128), f32),
            pltpu.VMEM((4, sources, width), f32),
            pltpu.VMEM((rows_all, 128), f32),
            pltpu.VMEM((rows_all, 128), f32),
            pltpu.VMEM((rows_all, 128), f32),
            pltpu.SMEM((TILE,), jnp.int32),
            pltpu.SMEM((TILE,), jnp.int32),
            pltpu.SemaphoreType.DMA((2,)),
        ],
        compiler_params=params,
        name="owner_forward",
    )(
        (sample_cells * 2).reshape(sources * width),
        arrived.reshape(4, sources, width),
        feature_grid[0],
        fine_in[0],
        fine_mid[0],
        fine_out,
        prop_in[0],
        prop_out,
    )
    ray_loss, in_sum, out_sum = pl.pallas_call(
        finish_kernel,
        out_shape=(
            jax.ShapeDtypeStruct((1, RAY_DEV), f32),
            jax.ShapeDtypeStruct((16, 32), f32),
            jax.ShapeDtypeStruct((1, 16), f32),
        ),
        in_specs=[vmem()] * 5 + [pl.BlockSpec(memory_space=pl.ANY)] * 2,
        out_specs=(vmem(), vmem(), vmem()),
        scratch_shapes=[
            pltpu.VMEM((sources, 2, 128), f32),
            pltpu.VMEM((sources, 1, 128), f32),
            pltpu.VMEM((sources, 1, 128), f32),
            pltpu.VMEM((lax.axis_size("rep"), 32, 128), f32),
            pltpu.VMEM((sources, 128), f32),
            pltpu.VMEM((slots, slots), bf16),
            pltpu.VMEM((rows_all, 128), f32),
            pltpu.VMEM((32, width), bf16),
            pltpu.VMEM((4, rows_all, 128), f32),
            pltpu.VMEM((sources, 48, width), bf16),
            pltpu.SemaphoreType.DMA((sources,)),
            pltpu.SemaphoreType.DMA((sources,)),
            pltpu.SemaphoreType.DMA((sources,)),
            pltpu.SemaphoreType.DMA((sources,)),
            pltpu.SemaphoreType.DMA((lax.axis_size("rep"),)),
            pltpu.SemaphoreType.DMA((lax.axis_size("rep"),)),
            pltpu.SemaphoreType.DMA((4,)),
        ],
        compiler_params=pltpu.CompilerParams(
            vmem_limit_bytes=58 * 2**20, collective_id=0, has_side_effects=True
        ),
        name="finish",
    )(
        stats,
        slot_ray[0, 0],
        slot_rank[0, 0],
        bucket_count[0],
        prop_out[0].astype(f32)[:, None],
        back,
        kept,
    )
    return (ray_loss.reshape(1, 1, -1), in_sum[None], out_sum)


def solution(mesh):
    return jax.shard_map(
        on_device,
        mesh=mesh,
        in_specs=(
            P("dom", None, None),
            P("dom", None, None),
            P("dom", None, None, None),
            P("dom", None),
            P("dom", None, None),
            P("dom", None),
            P("dom", "rep", None, None),
            P(None, "dom", "rep", None, None),
            P("dom", "rep", None, None),
            P("dom", "rep", None, None),
            P("dom", "rep", None),
        ),
        out_specs=(P("dom", "rep", None), P("dom", None, None), P("dom", None)),
        check_vma=False,
    )
```

```python
import functools

import jax
import jax.numpy as jnp
from jax import lax
from jax.experimental import pallas as pl
from jax.experimental.pallas import tpu as pltpu
from jax.sharding import PartitionSpec as P

GR = 32
RAY_DEV = 256
TILE = 1024
PART = 256
SHARES = (0, 128, 384, 640, 896, 1024)

distill_weight = 50.0
f32 = jnp.float32
bf16 = jnp.bfloat16
LANES_BOTH = (((1,), (1,)), ((), ()))
MESH = pl.DeviceIdType.MESH


def softplus(x):
    return jnp.maximum(x, 0.0) + jnp.log1p(jnp.exp(-jnp.abs(x)))


def group_total(x):
    once = x + pltpu.roll(x, 32, 1)
    return once + pltpu.roll(once, 64, 1)


def scan_segment(x, rows, forward):
    lane = lax.broadcasted_iota(jnp.int32, x.shape, 1)
    row = lax.broadcasted_iota(jnp.int32, x.shape, 0) % rows
    height = x.shape[0]

    def moved(value, step, axis):
        size = height if axis == 0 else 128
        return pltpu.roll(value, step if forward else size - step, axis)

    within = x
    for step in (32, 64):
        keep = lane >= step if forward else lane < 128 - step
        within = within + jnp.where(keep, moved(within, step, 1), 0.0)
    total = group_total(x)
    running = total
    step = 1
    while step < rows:
        keep = row >= step if forward else row < rows - step
        running = running + jnp.where(keep, moved(running, step, 0), 0.0)
        step *= 2
    edge = row >= 1 if forward else row < rows - 1
    return within + jnp.where(edge, moved(running, 1, 0), 0.0), total


def owner_kernel(
    cells_ref, geom_ref, grid_ref, fine_in_ref, fine_mid_ref, fine_out_ref, prop_in_ref, prop_out_ref,
    kept_ref, back_ref, stats_ref,
    table, even, odd, geo, fine_logit, prop_logit, spacing, even_cells, odd_cells, sems,
    first_all, mid_all, fine_head, prop_head, even_hold, odd_hold,
):
    sources, width = geom_ref.shape[1:]
    tiles_per = width // TILE
    tile_total = sources * tiles_per
    cell_blocks = grid_ref.shape[1] // 128
    rows_per = width // 128

    geo[...] = geom_ref[...].astype(f32)
    lane = lax.broadcasted_iota(jnp.int32, (GR, 128), 1)

    shifts = (1, GR, GR + 1)

    def block_of(block):
        here = grid_ref[:, pl.ds(pl.multiple_of(block * 128, 128), 128)].astype(f32)
        return (here,) + tuple(pltpu.roll(here, 128 - shift, 1) for shift in shifts)

    def build(second, block, here):
        there = block_of(jnp.minimum(block + 1, cell_blocks - 1))
        pieces = [here[0]]
        for index, shift in enumerate(shifts):
            pieces.append(jnp.where(lane < 128 - shift, here[index + 1], there[index + 1]))
        turned = jnp.transpose(jnp.concatenate(pieces, axis=0).astype(bf16)).astype(f32)
        table[pl.ds(pl.multiple_of(block * 256, 256), 128, stride=2), :] = turned
        if second:
            earlier = pl.multiple_of((block - GR * GR // 128) * 256, 256)
            table[pl.ds(earlier + 1, 128, stride=2), :] = turned
        return there

    slab = GR * GR // 128
    state = lax.fori_loop(0, slab, functools.partial(build, False), block_of(0))
    lax.fori_loop(slab, cell_blocks, functools.partial(build, True), state, unroll=4)

    hidden = fine_in_ref.shape[0]
    groups = TILE // PART

    def diagonal(weights):
        rows, columns = weights.shape
        wide = jnp.concatenate([weights.astype(f32)] * groups, axis=1)
        tall = jnp.concatenate([wide] * groups, axis=0)
        row = lax.broadcasted_iota(jnp.int32, tall.shape, 0) // rows
        column = lax.broadcasted_iota(jnp.int32, tall.shape, 1) // columns
        return jnp.where(row == column, tall, 0.0)

    def heads(weights):
        columns = weights.shape[1]
        wide = jnp.concatenate([weights.astype(f32)] * groups, axis=1)
        tall = jnp.broadcast_to(wide, (16, wide.shape[1]))
        row = lax.broadcasted_iota(jnp.int32, tall.shape, 0)
        column = lax.broadcasted_iota(jnp.int32, tall.shape, 1) // columns
        return jnp.where(row == column, tall, 0.0).astype(bf16)

    first_all[pl.ds(0, groups * hidden), :] = diagonal(fine_in_ref[...]).astype(bf16)
    first_all[pl.ds(groups * hidden, groups * 16), :] = diagonal(prop_in_ref[...]).astype(bf16)
    for layer in range(fine_mid_ref.shape[0]):
        mid_all[layer] = diagonal(fine_mid_ref[layer]).astype(bf16)
    fine_head[...] = heads(fine_out_ref[...])
    prop_head[...] = heads(prop_out_ref[...])
    eye = (
        lax.broadcasted_iota(jnp.int32, (256, 256), 0)
        == lax.broadcasted_iota(jnp.int32, (256, 256), 1)
    ).astype(f32).astype(bf16)

    def fetch(tile, indices, sem):
        start = pl.multiple_of(jnp.minimum(tile, tile_total - 1) * TILE, TILE)
        return pltpu.make_async_copy(cells_ref.at[pl.ds(start, TILE)], indices, sem)

    def gather(indices, low, start=0, stop=TILE):
        for j in range(start, stop):
            cell = pl.multiple_of(indices[j], 2)
            low[pl.ds(2 * j, 2), :] = table[pl.ds(cell, 2), :]

    def interpolate(tile, low, hold):
        source = tile // tiles_per
        first_lane = (tile % tiles_per) * TILE
        places = [
            pl.ds(pl.multiple_of(first_lane + part * PART, PART), PART) for part in range(groups)
        ]
        waiting = []
        for part in range(groups + 1):
            if part < groups:
                start = 2 * part * PART
                rows = jnp.concatenate(
                    [
                        low[pl.ds(start, PART, stride=2), :],
                        low[pl.ds(start + 1, PART, stride=2), :],
                    ],
                    axis=1,
                ).astype(bf16)
                waiting.append(
                    lax.dot_general(eye, rows, LANES_BOTH, preferred_element_type=f32)
                )
            if part > 0:
                lanes = places[part - 1]
                turned = waiting[part - 1]
                offsets = [geo[axis, pl.ds(source, 1), lanes] for axis in range(3)]
                factors = [[1.0 - value, value] for value in offsets]
                summed = jnp.zeros((32, PART), f32)
                for corner in range(8):
                    factor = (
                        factors[0][corner // 4]
                        * factors[1][corner // 2 % 2]
                        * factors[2][corner % 2]
                    )
                    summed = summed + turned[corner * 32 : (corner + 1) * 32] * factor
                features = summed.astype(bf16)
                kept_ref[source, pl.ds(0, 32), lanes] = features
                hold[pl.ds((part - 1) * 32, 32), :] = features
            yield

    def networks(tile, hold):
        source = tile // tiles_per
        first_lane = (tile % tiles_per) * TILE
        places = [
            pl.ds(pl.multiple_of(first_lane + part * PART, PART), PART) for part in range(groups)
        ]
        both = jnp.maximum(
            jnp.dot(first_all[...], hold[...], preferred_element_type=f32), 0.0
        ).astype(bf16)
        fine_hidden = both[: groups * hidden]
        prop_hidden = both[groups * hidden :]
        for part in range(groups):
            kept_ref[source, pl.ds(32, 16), places[part]] = prop_hidden[
                part * 16 : (part + 1) * 16
            ]
        yield
        for layer in range(fine_mid_ref.shape[0]):
            fine_hidden = jnp.maximum(
                jnp.dot(mid_all[layer], fine_hidden, preferred_element_type=f32), 0.0
            ).astype(bf16)
            yield
        fine = jnp.dot(fine_head[...], fine_hidden, preferred_element_type=f32)
        prop = jnp.dot(prop_head[...], prop_hidden, preferred_element_type=f32)
        for part in range(groups):
            gap = geo[3, pl.ds(source, 1), places[part]]
            for piece in range(PART // 128):
                row = pl.ds(tile * (TILE // 128) + (part * PART) // 128 + piece, 1)
                cut = slice(piece * 128, (piece + 1) * 128)
                fine_logit[row, :] = fine[part : part + 1, cut]
                prop_logit[row, :] = prop[part : part + 1, cut]
                spacing[row, :] = gap[:, cut]
        yield

    def weave(indices, into, tile, out_of, hold_now, hold_last):
        slots = groups + 1
        ahead = networks(jnp.maximum(tile - 1, 0), hold_last)
        now = interpolate(tile, out_of, hold_now)
        for slot in range(slots):
            gather(indices, into, SHARES[slot], SHARES[slot + 1])
            next(ahead, None)
            next(now, None)
        for unused in ahead:
            pass

    fetch(0, even_cells, sems.at[0]).start()
    fetch(1, odd_cells, sems.at[1]).start()
    fetch(0, even_cells, sems.at[0]).wait()
    gather(even_cells, even)

    def step(tile, carry):
        @pl.when(tile % 2 == 0)
        def _():
            fetch(tile + 2, even_cells, sems.at[0]).start()
            fetch(tile + 1, odd_cells, sems.at[1]).wait()
            weave(odd_cells, odd, tile, even, even_hold, odd_hold)

        @pl.when(tile % 2 == 1)
        def _():
            fetch(tile + 2, odd_cells, sems.at[1]).start()
            fetch(tile + 1, even_cells, sems.at[0]).wait()
            weave(even_cells, even, tile, odd, odd_hold, even_hold)

        return carry

    lax.fori_loop(0, tile_total, step, 0)
    fetch(tile_total, odd_cells, sems.at[1]).wait()
    for unused in networks(tile_total - 1, odd_hold):
        pass

    gap = spacing[...]
    prop_raw = prop_logit[...]
    optical = softplus(prop_raw) * gap
    depth, prop_total = scan_segment(optical, rows_per, True)
    before = jnp.exp(optical - depth)
    prop_taken = before - jnp.exp(-depth)
    back_ref[0] = prop_taken
    back_ref[1] = before
    back_ref[2] = gap * jax.nn.sigmoid(prop_raw)
    fine_optical = softplus(fine_logit[...]) * gap
    fine_depth, fine_total = scan_segment(fine_optical, rows_per, True)
    fine_taken = jnp.exp(fine_optical - fine_depth) - jnp.exp(-fine_depth)
    back_ref[3] = fine_taken

    def per_segment(value, totalled):
        over_rows = jnp.sum(value.reshape(sources, rows_per, 128), axis=1)
        return over_rows if totalled else group_total(over_rows)

    sum_aa = per_segment(prop_taken * prop_taken, False)
    sum_ab = per_segment(prop_taken * fine_taken, False)
    sum_bb = per_segment(fine_taken * fine_taken, False)
    log_prop = -per_segment(prop_total, True)
    log_fine = -per_segment(fine_total, True)
    part = lax.broadcasted_iota(jnp.int32, (sources, 128), 1) // 32
    stats_ref[:, 0, :] = jnp.where(
        part == 0, sum_aa, jnp.where(part == 1, sum_ab, jnp.where(part == 2, sum_bb, log_prop))
    )
    stats_ref[:, 1, :] = log_fine


def split_three(value):
    high = value.astype(bf16)
    rest = value - high.astype(f32)
    middle = rest.astype(bf16)
    low = (rest - middle.astype(f32)).astype(bf16)
    return [high, middle, low]


def finish_kernel(
    stats_ref, ray_ref, rank_ref, count_ref, prop_out_ref, back_hbm, kept_hbm,
    loss_ref, in_ref, out_ref,
    stats_in, factors_out, factors_in, grads_in, flat, ahead, logit_grad, left, back_ref, kept_ref,
    stats_send, stats_recv, factors_send, factors_recv, grads_send, grads_recv, local,
):
    sources, rows_kept, width = kept_ref.shape
    rows_per = width // 128
    slots = ahead.shape[0]
    blocks = slots // 128
    me, replica = lax.axis_index("dom"), lax.axis_index("rep")
    replicas = lax.axis_size("rep")

    load_kept = pltpu.make_async_copy(kept_hbm, kept_ref, local.at[0])
    load_back = pltpu.make_async_copy(back_hbm, back_ref, local.at[1])
    load_back.start()
    load_kept.start()

    barrier = pltpu.get_barrier_semaphore()

    def greet(step, carry):
        peer = lax.rem(me + step, sources)
        pl.semaphore_signal(barrier, inc=1, device_id=(peer, replica), device_id_type=MESH)
        return carry

    lax.fori_loop(1, sources, greet, 0)
    for step in range(1, replicas):
        other = lax.rem(replica + step, replicas)
        pl.semaphore_signal(barrier, inc=1, device_id=(me, other), device_id_type=MESH)
    pl.semaphore_wait(barrier, sources + replicas - 2)

    def exchange(source, target, send, recv):
        def copy(step):
            peer = lax.rem(me + step, sources)
            return pltpu.make_async_remote_copy(
                src_ref=source.at[peer],
                dst_ref=target.at[me],
                send_sem=send.at[step],
                recv_sem=recv.at[step],
                device_id=(peer, replica),
                device_id_type=MESH,
            )

        def start(step, carry):
            copy(step).start()
            return carry

        def finish(step, carry):
            copy(step).wait()
            return carry

        lax.fori_loop(1, sources, start, 0)
        return lambda: lax.fori_loop(1, sources, finish, 0)

    wait_stats = exchange(stats_ref, stats_in, stats_send, stats_recv)
    own_stats = pltpu.make_async_copy(stats_ref.at[me], stats_in.at[me], local.at[2])
    own_stats.start()

    part_row = lax.broadcasted_iota(jnp.int32, (sources, 128), 0)
    group = lax.broadcasted_iota(jnp.int32, (sources, 128), 1) // 32
    seat = part_row % 4
    fold = jnp.where(
        lax.broadcasted_iota(jnp.int32, (blocks, sources), 0)
        == lax.broadcasted_iota(jnp.int32, (blocks, sources), 1) // 4,
        1.0,
        0.0,
    )
    unfold = jnp.where(
        lax.broadcasted_iota(jnp.int32, (sources, blocks), 0) // 4
        == lax.broadcasted_iota(jnp.int32, (sources, blocks), 1),
        1.0,
        0.0,
    )

    def exact(first, second):
        return jnp.dot(first, second, precision=lax.Precision.HIGHEST, preferred_element_type=f32)

    def dense(seated):
        return exact(fold, jnp.where(group == seat, seated, 0.0))

    def four(value):
        return jnp.concatenate([value] * 4, axis=1)

    def as_row(value):
        return jnp.concatenate([value[b : b + 1] for b in range(blocks)], axis=1)

    def as_dense(value):
        return jnp.concatenate(
            [value[:, b * 128 : (b + 1) * 128] for b in range(blocks)], axis=0
        )

    counts = jnp.broadcast_to(count_ref[...].astype(f32), (sources, sources))
    diagonal = lax.broadcasted_iota(jnp.int32, (sources, sources), 0) == lax.broadcasted_iota(
        jnp.int32, (sources, sources), 1
    )
    count_column = jnp.sum(jnp.where(diagonal, counts, 0.0), axis=1, keepdims=True)
    slot_lane = (lax.broadcasted_iota(jnp.int32, (sources, 128), 1) % 32).astype(f32)
    live = as_row(dense(jnp.where(slot_lane < count_column, 1.0, 0.0)))
    rays = dense(four(ray_ref[...].astype(f32)))
    ranks = dense(four(rank_ref[...].astype(f32)))
    keys = rays * 64.0 + ranks
    key_row, rank_row = as_row(keys), as_row(ranks)
    key_column, ray_column = jnp.transpose(keys), jnp.transpose(rays)
    for chunk in range(blocks):
        gap = key_row - key_column[:, chunk : chunk + 1]
        ahead[pl.ds(chunk * 128, 128), :] = jnp.where(
            (gap > 0.5) & (gap < rank_row + 0.5), 1.0, 0.0
        ).astype(bf16)

    own_stats.wait()
    wait_stats()

    for index in range(sources):
        flat[pl.ds(index, 1), :] = stats_in[index, pl.ds(0, 1), :]
    packed = flat[...]
    turned = [packed] + [pltpu.roll(packed, 32 * step, 1) for step in range(1, 4)]

    def stat(index):
        value = turned[(3 - index) % 4]
        for place in range(3):
            value = jnp.where(seat == place, turned[(place - index) % 4], value)
        return as_row(dense(value))

    sum_aa, sum_ab, sum_bb, log_prop = (stat(index) for index in range(4))
    for index in range(sources):
        flat[pl.ds(index, 1), :] = stats_in[index, pl.ds(1, 1), :]
    log_fine = as_row(dense(flat[...]))

    def stacked(values):
        pieces = [piece.astype(f32) for value in values for piece in split_three(value)]
        pieces += [jnp.zeros_like(pieces[0])] * (8 - len(pieces))
        return jnp.concatenate(pieces, axis=0).astype(bf16)

    logs = stacked([log_prop * live, log_fine * live])
    reached = jnp.dot(logs, ahead[...], preferred_element_type=f32)
    entry_prop = jnp.exp(reached[0:1] + reached[1:2] + reached[2:3]) * live
    entry_fine = jnp.exp(reached[3:4] + reached[4:5] + reached[5:6]) * live
    slot_grad = distill_weight * (entry_prop * sum_aa - entry_fine * sum_ab) * entry_prop
    carried = lax.dot_general(
        stacked([slot_grad]), ahead[...], LANES_BOTH, preferred_element_type=f32
    )
    outgoing = (
        0.5 * distill_weight * entry_prop * entry_prop,
        -distill_weight * entry_prop * entry_fine,
        (carried[0:1] + carried[1:2] + carried[2:3]) * live,
    )
    message = jnp.zeros((sources, 128), f32)
    for index, value in enumerate(outgoing):
        spread = exact(unfold, as_dense(value))
        for place in range(4):
            shift = 32 * ((index - place) % 4)
            moved = pltpu.roll(spread, shift, 1) if shift else spread
            message = jnp.where((group == index) & (seat == place), moved, message)
    for index in range(sources):
        factors_out[index] = message[index : index + 1]

    wait_factors = exchange(factors_out, factors_in, factors_send, factors_recv)
    own_factors = pltpu.make_async_copy(factors_out.at[me], factors_in.at[me], local.at[3])
    own_factors.start()

    seg_loss = (
        entry_prop * entry_prop * sum_aa
        - 2.0 * entry_prop * entry_fine * sum_ab
        + entry_fine * entry_fine * sum_bb
    )
    losses = stacked([seg_loss])
    ray_loss = jnp.zeros((8, RAY_DEV), f32)
    ray_ids = lax.broadcasted_iota(jnp.int32, (128, RAY_DEV), 1).astype(f32)
    for chunk in range(blocks):
        mask = jnp.where(ray_column[:, chunk : chunk + 1] == ray_ids, 1.0, 0.0).astype(bf16)
        ray_loss = ray_loss + jnp.dot(
            losses[:, chunk * 128 : (chunk + 1) * 128], mask, preferred_element_type=f32
        )
    loss_ref[...] = 0.5 * distill_weight * (ray_loss[0:1] + ray_loss[1:2] + ray_loss[2:3])

    load_back.wait()
    load_kept.wait()
    own_factors.wait()
    wait_factors()

    for index in range(sources):
        flat[pl.ds(index, 1), :] = factors_in[index]
    factors = flat[...]

    def to_samples(index):
        spread = group_total(jnp.where(group == index, factors, 0.0))
        return jnp.broadcast_to(spread[:, None, :], (sources, rows_per, 128)).reshape(
            sources * rows_per, 128
        )

    taken = back_ref[0]
    taken_grad = 2.0 * to_samples(0) * taken + to_samples(1) * back_ref[3]
    behind, unused = scan_segment(taken_grad * taken, rows_per, False)
    grad = (taken_grad * back_ref[1] - behind - to_samples(2)) * back_ref[2]
    logit_grad[...] = grad.astype(bf16).astype(f32)

    def accumulate(source, total):
        for part_index in range(rows_per):
            lanes = pl.ds(part_index * 128, 128)
            row = logit_grad[pl.ds(source * rows_per + part_index, 1), :]
            hidden = kept_ref[source, pl.ds(32, 16), lanes].astype(f32)
            wide = jnp.broadcast_to(row, (16, 128))
            left[pl.ds(0, 16), lanes] = jnp.where(hidden > 0, wide, 0.0).astype(bf16)
            left[pl.ds(16, 16), lanes] = wide.astype(bf16)
        return total + lax.dot_general(
            left[...], kept_ref[source], LANES_BOTH, preferred_element_type=f32
        )

    total = lax.fori_loop(0, sources, accumulate, jnp.zeros((32, rows_kept), f32))
    grads_in[replica] = jnp.concatenate([total, jnp.zeros((32, 128 - rows_kept), f32)], axis=1)

    def share(step):
        other = lax.rem(replica + step, replicas)
        return pltpu.make_async_remote_copy(
            src_ref=grads_in.at[replica],
            dst_ref=grads_in.at[replica],
            send_sem=grads_send.at[step],
            recv_sem=grads_recv.at[step],
            device_id=(me, other),
            device_id_type=MESH,
        )

    for step in range(1, replicas):
        share(step).start()
    for step in range(1, replicas):
        share(step).wait()
    summed = grads_in[0]
    for index in range(1, replicas):
        summed = summed + grads_in[index]
    in_ref[...] = summed[0:16, 0:32] * prop_out_ref[...]
    out_ref[...] = summed[16:17, 32:48]


def vmem():
    return pl.BlockSpec(memory_space=pltpu.VMEM)


def on_device(
    feature_grid,
    fine_in,
    fine_mid,
    fine_out,
    prop_in,
    prop_out,
    sample_cells,
    sample_geometry,
    slot_ray,
    slot_rank,
    bucket_count,
):
    sources = lax.axis_size("dom")
    capacity = slot_ray.shape[3]
    width = sample_cells.shape[3]
    rows_all = sources * width // 128
    slots = sources * capacity
    cell_total = feature_grid.shape[2]
    params = pltpu.CompilerParams(vmem_limit_bytes=58 * 2**20)

    arrived = lax.all_to_all(sample_geometry, "dom", split_axis=3, concat_axis=3, tiled=True)
    kept, back, stats = pl.pallas_call(
        owner_kernel,
        out_shape=(
            jax.ShapeDtypeStruct((sources, 48, width), bf16),
            jax.ShapeDtypeStruct((4, rows_all, 128), f32),
            jax.ShapeDtypeStruct((sources, 2, 128), f32),
        ),
        in_specs=[pl.BlockSpec(memory_space=pl.ANY)] + [vmem()] * 7,
        out_specs=(vmem(), vmem(), vmem()),
        scratch_shapes=[
            pltpu.VMEM((2 * cell_total, 128), f32),
            pltpu.VMEM((2 * TILE, 128), f32),
            pltpu.VMEM((2 * TILE, 128), f32),
            pltpu.VMEM((4, sources, width), f32),
            pltpu.VMEM((rows_all, 128), f32),
            pltpu.VMEM((rows_all, 128), f32),
            pltpu.VMEM((rows_all, 128), f32),
            pltpu.SMEM((TILE,), jnp.int32),
            pltpu.SMEM((TILE,), jnp.int32),
            pltpu.SemaphoreType.DMA((2,)),
            pltpu.VMEM((TILE // PART * 80, TILE // PART * 32), bf16),
            pltpu.VMEM((fine_mid.shape[1], TILE // PART * 64, TILE // PART * 64), bf16),
            pltpu.VMEM((16, TILE // PART * 64), bf16),
            pltpu.VMEM((16, TILE // PART * 16), bf16),
            pltpu.VMEM((TILE // PART * 32, PART), bf16),
            pltpu.VMEM((TILE // PART * 32, PART), bf16),
        ],
        compiler_params=params,
        name="owner_forward",
    )(
        (sample_cells * 2).reshape(sources * width),
        arrived.reshape(4, sources, width),
        feature_grid[0],
        fine_in[0],
        fine_mid[0],
        fine_out,
        prop_in[0],
        prop_out,
    )
    ray_loss, in_sum, out_sum = pl.pallas_call(
        finish_kernel,
        out_shape=(
            jax.ShapeDtypeStruct((1, RAY_DEV), f32),
            jax.ShapeDtypeStruct((16, 32), f32),
            jax.ShapeDtypeStruct((1, 16), f32),
        ),
        in_specs=[vmem()] * 5 + [pl.BlockSpec(memory_space=pl.ANY)] * 2,
        out_specs=(vmem(), vmem(), vmem()),
        scratch_shapes=[
            pltpu.VMEM((sources, 2, 128), f32),
            pltpu.VMEM((sources, 1, 128), f32),
            pltpu.VMEM((sources, 1, 128), f32),
            pltpu.VMEM((lax.axis_size("rep"), 32, 128), f32),
            pltpu.VMEM((sources, 128), f32),
            pltpu.VMEM((slots, slots), bf16),
            pltpu.VMEM((rows_all, 128), f32),
            pltpu.VMEM((32, width), bf16),
            pltpu.VMEM((4, rows_all, 128), f32),
            pltpu.VMEM((sources, 48, width), bf16),
            pltpu.SemaphoreType.DMA((sources,)),
            pltpu.SemaphoreType.DMA((sources,)),
            pltpu.SemaphoreType.DMA((sources,)),
            pltpu.SemaphoreType.DMA((sources,)),
            pltpu.SemaphoreType.DMA((lax.axis_size("rep"),)),
            pltpu.SemaphoreType.DMA((lax.axis_size("rep"),)),
            pltpu.SemaphoreType.DMA((4,)),
        ],
        compiler_params=pltpu.CompilerParams(
            vmem_limit_bytes=58 * 2**20, collective_id=0, has_side_effects=True
        ),
        name="finish",
    )(
        stats,
        slot_ray[0, 0],
        slot_rank[0, 0],
        bucket_count[0],
        prop_out[0].astype(f32)[:, None],
        back,
        kept,
    )
    return (ray_loss.reshape(1, 1, -1), in_sum[None], out_sum)


def solution(mesh):
    return jax.shard_map(
        on_device,
        mesh=mesh,
        in_specs=(
            P("dom", None, None),
            P("dom", None, None),
            P("dom", None, None, None),
            P("dom", None),
            P("dom", None, None),
            P("dom", None),
            P("dom", "rep", None, None),
            P(None, "dom", "rep", None, None),
            P("dom", "rep", None, None),
            P("dom", "rep", None, None),
            P("dom", "rep", None),
        ),
        out_specs=(P("dom", "rep", None), P("dom", None, None), P("dom", None)),
        check_vma=False,
    )
```

```python
import functools

import jax
import jax.numpy as jnp
from jax import lax
from jax.experimental import pallas as pl
from jax.experimental.pallas import tpu as pltpu
from jax.sharding import PartitionSpec as P

GR = 32
RAY_DEV = 256
TILE = 1024
PIECES = 4
PART = 256
SHARES = (0, 128, 384, 640, 896, 1024)

distill_weight = 50.0
f32 = jnp.float32
bf16 = jnp.bfloat16
LANES_BOTH = (((1,), (1,)), ((), ()))
MESH = pl.DeviceIdType.MESH


def softplus(x):
    return jnp.maximum(x, 0.0) + jnp.log1p(jnp.exp(-jnp.abs(x)))


def group_total(x):
    once = x + pltpu.roll(x, 32, 1)
    return once + pltpu.roll(once, 64, 1)


def scan_segment(x, rows, forward):
    lane = lax.broadcasted_iota(jnp.int32, x.shape, 1)
    row = lax.broadcasted_iota(jnp.int32, x.shape, 0) % rows
    height = x.shape[0]

    def moved(value, step, axis):
        size = height if axis == 0 else 128
        return pltpu.roll(value, step if forward else size - step, axis)

    within = x
    for step in (32, 64):
        keep = lane >= step if forward else lane < 128 - step
        within = within + jnp.where(keep, moved(within, step, 1), 0.0)
    total = group_total(x)
    running = total
    step = 1
    while step < rows:
        keep = row >= step if forward else row < rows - step
        running = running + jnp.where(keep, moved(running, step, 0), 0.0)
        step *= 2
    edge = row >= 1 if forward else row < rows - 1
    return within + jnp.where(edge, moved(running, 1, 0), 0.0), total


def scatter_kernel(geom_ref, grid_ref, geo_ref, table_hbm, arrived, table, send, recv, local):
    sources = geom_ref.shape[0]
    cell_blocks = grid_ref.shape[1] // 128
    me, replica = lax.axis_index("dom"), lax.axis_index("rep")
    barrier = pltpu.get_barrier_semaphore()

    def greet(step, carry):
        peer = lax.rem(me + step, sources)
        pl.semaphore_signal(barrier, inc=1, device_id=(peer, replica), device_id_type=MESH)
        return carry

    lax.fori_loop(1, sources, greet, 0)
    pl.semaphore_wait(barrier, sources - 1)

    def copy(step):
        peer = lax.rem(me + step, sources)
        return pltpu.make_async_remote_copy(
            src_ref=geom_ref.at[peer],
            dst_ref=arrived.at[me],
            send_sem=send.at[step],
            recv_sem=recv.at[step],
            device_id=(peer, replica),
            device_id_type=MESH,
        )

    def start(step, carry):
        copy(step).start()
        return carry

    def finish(step, carry):
        copy(step).wait()
        return carry

    lax.fori_loop(1, sources, start, 0)
    own = pltpu.make_async_copy(geom_ref.at[me], arrived.at[me], local.at[PIECES])
    own.start()

    lane = lax.broadcasted_iota(jnp.int32, (GR, 128), 1)
    shifts = (1, GR, GR + 1)

    def block_of(block):
        here = grid_ref[:, pl.ds(pl.multiple_of(block * 128, 128), 128)].astype(f32)
        return (here,) + tuple(pltpu.roll(here, 128 - shift, 1) for shift in shifts)

    def build(block, here):
        there = block_of(jnp.minimum(block + 1, cell_blocks - 1))
        pieces = [here[0]]
        for index, shift in enumerate(shifts):
            pieces.append(jnp.where(lane < 128 - shift, here[index + 1], there[index + 1]))
        table[pl.ds(pl.multiple_of(block * 128, 128), 128), :] = jnp.transpose(
            jnp.concatenate(pieces, axis=0).astype(bf16)
        )
        return there

    state = block_of(0)
    per_piece = cell_blocks // PIECES
    for piece in range(PIECES):
        state = lax.fori_loop(
            piece * per_piece, (piece + 1) * per_piece, build, state, unroll=4
        )
        table_piece(table, table_hbm, local, piece).start()
    own.wait()
    lax.fori_loop(1, sources, finish, 0)
    geo_ref[...] = arrived[...].astype(f32)
    for piece in range(PIECES):
        table_piece(table, table_hbm, local, piece).wait()


def table_piece(source, target, sems, piece):
    height = source.shape[0] // PIECES
    rows = pl.ds(piece * height, height)
    return pltpu.make_async_copy(source.at[rows], target.at[rows], sems.at[piece])


def owner_kernel(
    cells_ref, geo, table_hbm, fine_in_ref, fine_mid_ref, fine_out_ref, prop_in_ref, prop_out_ref,
    kept_hbm, back_ref, stats_ref,
    kept_ref, kept_sems, narrow, table, even, odd, fine_logit, prop_logit, spacing, even_cells, odd_cells, sems,
    first_all, mid_all, fine_head, prop_head, even_hold, odd_hold,
):
    sources, rows_kept, width = kept_ref.shape
    tiles_per = width // TILE
    tile_total = sources * tiles_per
    rows_per = width // 128
    for piece in range(PIECES):
        table_piece(table_hbm, narrow, kept_sems, piece).start()

    hidden = fine_in_ref.shape[0]
    groups = TILE // PART

    def diagonal(weights):
        rows, columns = weights.shape
        wide = jnp.concatenate([weights.astype(f32)] * groups, axis=1)
        tall = jnp.concatenate([wide] * groups, axis=0)
        row = lax.broadcasted_iota(jnp.int32, tall.shape, 0) // rows
        column = lax.broadcasted_iota(jnp.int32, tall.shape, 1) // columns
        return jnp.where(row == column, tall, 0.0)

    def heads(weights):
        columns = weights.shape[1]
        wide = jnp.concatenate([weights.astype(f32)] * groups, axis=1)
        tall = jnp.broadcast_to(wide, (16, wide.shape[1]))
        row = lax.broadcasted_iota(jnp.int32, tall.shape, 0)
        column = lax.broadcasted_iota(jnp.int32, tall.shape, 1) // columns
        return jnp.where(row == column, tall, 0.0).astype(bf16)

    first_all[pl.ds(0, groups * hidden), :] = diagonal(fine_in_ref[...]).astype(bf16)
    first_all[pl.ds(groups * hidden, groups * 16), :] = diagonal(prop_in_ref[...]).astype(bf16)
    for layer in range(fine_mid_ref.shape[0]):
        mid_all[layer] = diagonal(fine_mid_ref[layer]).astype(bf16)
    fine_head[...] = heads(fine_out_ref[...])
    prop_head[...] = heads(prop_out_ref[...])
    eye = (
        lax.broadcasted_iota(jnp.int32, (256, 256), 0)
        == lax.broadcasted_iota(jnp.int32, (256, 256), 1)
    ).astype(f32).astype(bf16)

    cell_blocks = table_hbm.shape[0] // 128
    slab = GR * GR // 128
    per_piece = cell_blocks // PIECES

    def widen(second, block, carry):
        rows = narrow[pl.ds(pl.multiple_of(block * 128, 128), 128), :].astype(f32)
        table[pl.ds(pl.multiple_of(block * 256, 256), 128, stride=2), :] = rows
        if second:
            earlier = pl.multiple_of((block - slab) * 256, 256)
            table[pl.ds(earlier + 1, 128, stride=2), :] = rows
        return carry

    for piece in range(PIECES):
        table_piece(table_hbm, narrow, kept_sems, piece).wait()
        low = piece * per_piece
        if piece == 0:
            lax.fori_loop(0, slab, functools.partial(widen, False), 0)
            low = slab
        lax.fori_loop(low, (piece + 1) * per_piece, functools.partial(widen, True), 0, unroll=4)

    def save(source):
        return pltpu.make_async_copy(
            kept_ref.at[source], kept_hbm.at[source], kept_sems.at[source]
        )

    def fetch(tile, indices, sem):
        start = pl.multiple_of(jnp.minimum(tile, tile_total - 1) * TILE, TILE)
        return pltpu.make_async_copy(cells_ref.at[pl.ds(start, TILE)], indices, sem)

    def gather(indices, low, start=0, stop=TILE):
        for j in range(start, stop):
            cell = pl.multiple_of(indices[j], 2)
            low[pl.ds(2 * j, 2), :] = table[pl.ds(cell, 2), :]

    def interpolate(tile, low, hold):
        source = tile // tiles_per
        first_lane = (tile % tiles_per) * TILE
        places = [
            pl.ds(pl.multiple_of(first_lane + part * PART, PART), PART) for part in range(groups)
        ]
        waiting = []
        for part in range(groups + 1):
            if part < groups:
                start = 2 * part * PART
                rows = jnp.concatenate(
                    [
                        low[pl.ds(start, PART, stride=2), :],
                        low[pl.ds(start + 1, PART, stride=2), :],
                    ],
                    axis=1,
                ).astype(bf16)
                waiting.append(
                    lax.dot_general(eye, rows, LANES_BOTH, preferred_element_type=f32)
                )
            if part > 0:
                lanes = places[part - 1]
                turned = waiting[part - 1]
                place = tile % tiles_per * (TILE // 128) + (part - 1) * (PART // 128)
                offsets = [
                    jnp.concatenate(
                        [
                            geo[source, pl.ds(axis * rows_per + place + piece, 1), :]
                            for piece in range(PART // 128)
                        ],
                        axis=1,
                    )
                    for axis in range(3)
                ]
                factors = [[1.0 - value, value] for value in offsets]
                summed = jnp.zeros((32, PART), f32)
                for corner in range(8):
                    factor = (
                        factors[0][corner // 4]
                        * factors[1][corner // 2 % 2]
                        * factors[2][corner % 2]
                    )
                    summed = summed + turned[corner * 32 : (corner + 1) * 32] * factor
                features = summed.astype(bf16)
                kept_ref[source, pl.ds(0, 32), lanes] = features
                hold[pl.ds((part - 1) * 32, 32), :] = features
            yield

    def networks(tile, hold):
        source = tile // tiles_per
        first_lane = (tile % tiles_per) * TILE
        places = [
            pl.ds(pl.multiple_of(first_lane + part * PART, PART), PART) for part in range(groups)
        ]
        both = jnp.maximum(
            jnp.dot(first_all[...], hold[...], preferred_element_type=f32), 0.0
        ).astype(bf16)
        fine_hidden = both[: groups * hidden]
        prop_hidden = both[groups * hidden :]
        for part in range(groups):
            kept_ref[source, pl.ds(32, 16), places[part]] = prop_hidden[
                part * 16 : (part + 1) * 16
            ]
        yield
        for layer in range(fine_mid_ref.shape[0]):
            fine_hidden = jnp.maximum(
                jnp.dot(mid_all[layer], fine_hidden, preferred_element_type=f32), 0.0
            ).astype(bf16)
            yield
        spacing[pl.ds(pl.multiple_of(tile * (TILE // 128), 8), TILE // 128), :] = geo[
            source,
            pl.ds(
                pl.multiple_of(3 * rows_per + tile % tiles_per * (TILE // 128), 8), TILE // 128
            ),
            :,
        ]
        fine = jnp.dot(fine_head[...], fine_hidden, preferred_element_type=f32)
        prop = jnp.dot(prop_head[...], prop_hidden, preferred_element_type=f32)
        for part in range(groups):
            for piece in range(PART // 128):
                row = pl.ds(tile * (TILE // 128) + (part * PART) // 128 + piece, 1)
                cut = slice(piece * 128, (piece + 1) * 128)
                fine_logit[row, :] = fine[part : part + 1, cut]
                prop_logit[row, :] = prop[part : part + 1, cut]
        yield

    def weave(indices, into, tile, out_of, hold_now, hold_last):
        slots = groups + 1
        ahead = networks(jnp.maximum(tile - 1, 0), hold_last)
        now = interpolate(tile, out_of, hold_now)
        for slot in range(slots):
            gather(indices, into, SHARES[slot], SHARES[slot + 1])
            next(ahead, None)
            next(now, None)
        for unused in ahead:
            pass

    fetch(0, even_cells, sems.at[0]).start()
    fetch(1, odd_cells, sems.at[1]).start()
    fetch(0, even_cells, sems.at[0]).wait()
    gather(even_cells, even)

    def step(tile, carry):
        @pl.when((tile % 2 == 0) & (tile >= 4))
        def _():
            save(tile // 2 - 2).start()

        @pl.when(tile % 2 == 0)
        def _():
            fetch(tile + 2, even_cells, sems.at[0]).start()
            fetch(tile + 1, odd_cells, sems.at[1]).wait()
            weave(odd_cells, odd, tile, even, even_hold, odd_hold)

        @pl.when(tile % 2 == 1)
        def _():
            fetch(tile + 2, odd_cells, sems.at[1]).start()
            fetch(tile + 1, even_cells, sems.at[0]).wait()
            weave(even_cells, even, tile, odd, odd_hold, even_hold)

        return carry

    lax.fori_loop(0, tile_total, step, 0)
    fetch(tile_total, odd_cells, sems.at[1]).wait()
    for unused in networks(tile_total - 1, odd_hold):
        pass

    save(sources - 2).start()
    save(sources - 1).start()

    gap = spacing[...]
    prop_raw = prop_logit[...]
    optical = softplus(prop_raw) * gap
    depth, prop_total = scan_segment(optical, rows_per, True)
    before = jnp.exp(optical - depth)
    prop_taken = before - jnp.exp(-depth)
    back_ref[0] = prop_taken
    back_ref[1] = before
    back_ref[2] = gap * jax.nn.sigmoid(prop_raw)
    fine_optical = softplus(fine_logit[...]) * gap
    fine_depth, fine_total = scan_segment(fine_optical, rows_per, True)
    fine_taken = jnp.exp(fine_optical - fine_depth) - jnp.exp(-fine_depth)
    back_ref[3] = fine_taken

    def per_segment(value, totalled):
        over_rows = jnp.sum(value.reshape(sources, rows_per, 128), axis=1)
        return over_rows if totalled else group_total(over_rows)

    sum_aa = per_segment(prop_taken * prop_taken, False)
    sum_ab = per_segment(prop_taken * fine_taken, False)
    sum_bb = per_segment(fine_taken * fine_taken, False)
    log_prop = -per_segment(prop_total, True)
    log_fine = -per_segment(fine_total, True)
    part = lax.broadcasted_iota(jnp.int32, (sources, 128), 1) // 32
    stats_ref[:, 0, :] = jnp.where(
        part == 0, sum_aa, jnp.where(part == 1, sum_ab, jnp.where(part == 2, sum_bb, log_prop))
    )
    stats_ref[:, 1, :] = log_fine

    def saved(source, carry):
        save(source).wait()
        return carry

    lax.fori_loop(0, sources, saved, 0)


def split_three(value):
    high = value.astype(bf16)
    rest = value - high.astype(f32)
    middle = rest.astype(bf16)
    low = (rest - middle.astype(f32)).astype(bf16)
    return [high, middle, low]


def finish_kernel(
    stats_ref, ray_ref, rank_ref, count_ref, prop_out_ref, back_hbm, kept_hbm,
    result_ref,
    stats_in, factors_out, factors_in, grads_in, flat, ahead, logit_grad, left, back_ref, kept_ref,
    stats_send, stats_recv, factors_send, factors_recv, grads_send, grads_recv, local,
):
    sources, rows_kept, width = kept_ref.shape
    rows_per = width // 128
    slots = ahead.shape[0]
    blocks = slots // 128
    me, replica = lax.axis_index("dom"), lax.axis_index("rep")
    replicas = lax.axis_size("rep")

    load_kept = pltpu.make_async_copy(kept_hbm, kept_ref, local.at[0])
    load_back = pltpu.make_async_copy(back_hbm, back_ref, local.at[1])
    load_back.start()
    load_kept.start()

    barrier = pltpu.get_barrier_semaphore()

    def greet(step, carry):
        peer = lax.rem(me + step, sources)
        pl.semaphore_signal(barrier, inc=1, device_id=(peer, replica), device_id_type=MESH)
        return carry

    lax.fori_loop(1, sources, greet, 0)
    for step in range(1, replicas):
        other = lax.rem(replica + step, replicas)
        pl.semaphore_signal(barrier, inc=1, device_id=(me, other), device_id_type=MESH)
    pl.semaphore_wait(barrier, sources + replicas - 2)

    def exchange(source, target, send, recv):
        def copy(step):
            peer = lax.rem(me + step, sources)
            return pltpu.make_async_remote_copy(
                src_ref=source.at[peer],
                dst_ref=target.at[me],
                send_sem=send.at[step],
                recv_sem=recv.at[step],
                device_id=(peer, replica),
                device_id_type=MESH,
            )

        def start(step, carry):
            copy(step).start()
            return carry

        def finish(step, carry):
            copy(step).wait()
            return carry

        lax.fori_loop(1, sources, start, 0)
        return lambda: lax.fori_loop(1, sources, finish, 0)

    wait_stats = exchange(stats_ref, stats_in, stats_send, stats_recv)
    own_stats = pltpu.make_async_copy(stats_ref.at[me], stats_in.at[me], local.at[2])
    own_stats.start()

    part_row = lax.broadcasted_iota(jnp.int32, (sources, 128), 0)
    group = lax.broadcasted_iota(jnp.int32, (sources, 128), 1) // 32
    seat = part_row % 4
    fold = jnp.where(
        lax.broadcasted_iota(jnp.int32, (blocks, sources), 0)
        == lax.broadcasted_iota(jnp.int32, (blocks, sources), 1) // 4,
        1.0,
        0.0,
    )
    unfold = jnp.where(
        lax.broadcasted_iota(jnp.int32, (sources, blocks), 0) // 4
        == lax.broadcasted_iota(jnp.int32, (sources, blocks), 1),
        1.0,
        0.0,
    )

    def exact(first, second):
        return jnp.dot(first, second, precision=lax.Precision.HIGHEST, preferred_element_type=f32)

    def dense(seated):
        return exact(fold, jnp.where(group == seat, seated, 0.0))

    def four(value):
        return jnp.concatenate([value] * 4, axis=1)

    def as_row(value):
        return jnp.concatenate([value[b : b + 1] for b in range(blocks)], axis=1)

    def as_dense(value):
        return jnp.concatenate(
            [value[:, b * 128 : (b + 1) * 128] for b in range(blocks)], axis=0
        )

    counts = jnp.broadcast_to(count_ref[...].astype(f32), (sources, sources))
    diagonal = lax.broadcasted_iota(jnp.int32, (sources, sources), 0) == lax.broadcasted_iota(
        jnp.int32, (sources, sources), 1
    )
    count_column = jnp.sum(jnp.where(diagonal, counts, 0.0), axis=1, keepdims=True)
    slot_lane = (lax.broadcasted_iota(jnp.int32, (sources, 128), 1) % 32).astype(f32)
    live = as_row(dense(jnp.where(slot_lane < count_column, 1.0, 0.0)))
    rays = dense(four(ray_ref[...].astype(f32)))
    ranks = dense(four(rank_ref[...].astype(f32)))
    keys = rays * 64.0 + ranks
    key_row, rank_row = as_row(keys), as_row(ranks)
    key_column, ray_column = jnp.transpose(keys), jnp.transpose(rays)
    for chunk in range(blocks):
        gap = key_row - key_column[:, chunk : chunk + 1]
        ahead[pl.ds(chunk * 128, 128), :] = jnp.where(
            (gap > 0.5) & (gap < rank_row + 0.5), 1.0, 0.0
        ).astype(bf16)

    own_stats.wait()
    wait_stats()

    for index in range(sources):
        flat[pl.ds(index, 1), :] = stats_in[index, pl.ds(0, 1), :]
    packed = flat[...]
    turned = [packed] + [pltpu.roll(packed, 32 * step, 1) for step in range(1, 4)]

    def stat(index):
        value = turned[(3 - index) % 4]
        for place in range(3):
            value = jnp.where(seat == place, turned[(place - index) % 4], value)
        return as_row(dense(value))

    sum_aa, sum_ab, sum_bb, log_prop = (stat(index) for index in range(4))
    for index in range(sources):
        flat[pl.ds(index, 1), :] = stats_in[index, pl.ds(1, 1), :]
    log_fine = as_row(dense(flat[...]))

    def stacked(values):
        pieces = [piece.astype(f32) for value in values for piece in split_three(value)]
        pieces += [jnp.zeros_like(pieces[0])] * (8 - len(pieces))
        return jnp.concatenate(pieces, axis=0).astype(bf16)

    logs = stacked([log_prop * live, log_fine * live])
    reached = jnp.dot(logs, ahead[...], preferred_element_type=f32)
    entry_prop = jnp.exp(reached[0:1] + reached[1:2] + reached[2:3]) * live
    entry_fine = jnp.exp(reached[3:4] + reached[4:5] + reached[5:6]) * live
    slot_grad = distill_weight * (entry_prop * sum_aa - entry_fine * sum_ab) * entry_prop
    carried = lax.dot_general(
        stacked([slot_grad]), ahead[...], LANES_BOTH, preferred_element_type=f32
    )
    outgoing = (
        0.5 * distill_weight * entry_prop * entry_prop,
        -distill_weight * entry_prop * entry_fine,
        (carried[0:1] + carried[1:2] + carried[2:3]) * live,
    )
    message = jnp.zeros((sources, 128), f32)
    for index, value in enumerate(outgoing):
        spread = exact(unfold, as_dense(value))
        for place in range(4):
            shift = 32 * ((index - place) % 4)
            moved = pltpu.roll(spread, shift, 1) if shift else spread
            message = jnp.where((group == index) & (seat == place), moved, message)
    for index in range(sources):
        factors_out[index] = message[index : index + 1]

    wait_factors = exchange(factors_out, factors_in, factors_send, factors_recv)
    own_factors = pltpu.make_async_copy(factors_out.at[me], factors_in.at[me], local.at[3])
    own_factors.start()

    seg_loss = (
        entry_prop * entry_prop * sum_aa
        - 2.0 * entry_prop * entry_fine * sum_ab
        + entry_fine * entry_fine * sum_bb
    )
    losses = stacked([seg_loss])
    ray_loss = jnp.zeros((8, RAY_DEV), f32)
    ray_ids = lax.broadcasted_iota(jnp.int32, (128, RAY_DEV), 1).astype(f32)
    for chunk in range(blocks):
        mask = jnp.where(ray_column[:, chunk : chunk + 1] == ray_ids, 1.0, 0.0).astype(bf16)
        ray_loss = ray_loss + jnp.dot(
            losses[:, chunk * 128 : (chunk + 1) * 128], mask, preferred_element_type=f32
        )
    ray_loss = 0.5 * distill_weight * (ray_loss[0:1] + ray_loss[1:2] + ray_loss[2:3])
    for index in range(RAY_DEV // 128):
        result_ref[pl.ds(32 + index, 1), :] = ray_loss[:, index * 128 : (index + 1) * 128]

    load_back.wait()
    load_kept.wait()
    own_factors.wait()
    wait_factors()

    for index in range(sources):
        flat[pl.ds(index, 1), :] = factors_in[index]
    factors = flat[...]

    def to_samples(index):
        spread = group_total(jnp.where(group == index, factors, 0.0))
        return jnp.broadcast_to(spread[:, None, :], (sources, rows_per, 128)).reshape(
            sources * rows_per, 128
        )

    taken = back_ref[0]
    taken_grad = 2.0 * to_samples(0) * taken + to_samples(1) * back_ref[3]
    behind, unused = scan_segment(taken_grad * taken, rows_per, False)
    grad = (taken_grad * back_ref[1] - behind - to_samples(2)) * back_ref[2]
    logit_grad[...] = grad.astype(bf16).astype(f32)

    def accumulate(source, total):
        for part_index in range(rows_per):
            lanes = pl.ds(part_index * 128, 128)
            row = logit_grad[pl.ds(source * rows_per + part_index, 1), :]
            hidden = kept_ref[source, pl.ds(32, 16), lanes].astype(f32)
            wide = jnp.broadcast_to(row, (16, 128))
            left[pl.ds(0, 16), lanes] = jnp.where(hidden > 0, wide, 0.0).astype(bf16)
            left[pl.ds(16, 16), lanes] = wide.astype(bf16)
        return total + lax.dot_general(
            left[...], kept_ref[source], LANES_BOTH, preferred_element_type=f32
        )

    total = lax.fori_loop(0, sources, accumulate, jnp.zeros((32, rows_kept), f32))
    grads_in[replica] = jnp.concatenate([total, jnp.zeros((32, 128 - rows_kept), f32)], axis=1)

    def share(step):
        other = lax.rem(replica + step, replicas)
        return pltpu.make_async_remote_copy(
            src_ref=grads_in.at[replica],
            dst_ref=grads_in.at[replica],
            send_sem=grads_send.at[step],
            recv_sem=grads_recv.at[step],
            device_id=(me, other),
            device_id_type=MESH,
        )

    for step in range(1, replicas):
        share(step).start()
    for step in range(1, replicas):
        share(step).wait()
    summed = grads_in[0]
    for index in range(1, replicas):
        summed = summed + grads_in[index]
    result_ref[pl.ds(0, 16), :] = summed[0:16] * prop_out_ref[...]
    result_ref[pl.ds(16, 16), :] = summed[16:32]


def vmem():
    return pl.BlockSpec(memory_space=pltpu.VMEM)


def on_device(
    feature_grid,
    fine_in,
    fine_mid,
    fine_out,
    prop_in,
    prop_out,
    sample_cells,
    sample_geometry,
    slot_ray,
    slot_rank,
    bucket_count,
):
    sources = lax.axis_size("dom")
    capacity = slot_ray.shape[3]
    width = sample_cells.shape[3]
    rows_all = sources * width // 128
    slots = sources * capacity
    cell_total = feature_grid.shape[2]
    params = pltpu.CompilerParams(vmem_limit_bytes=60 * 2**20)

    by_part = (
        sample_geometry.reshape(4, sources, width)
        .transpose(1, 0, 2)
        .reshape(sources, 4 * width // 128, 128)
    )
    geometry, corners = pl.pallas_call(
        scatter_kernel,
        out_shape=(
            jax.ShapeDtypeStruct(by_part.shape, f32),
            jax.ShapeDtypeStruct((cell_total, 128), bf16),
        ),
        in_specs=[vmem()] * 2,
        out_specs=(vmem(), pl.BlockSpec(memory_space=pl.ANY)),
        scratch_shapes=[
            pltpu.VMEM(by_part.shape, bf16),
            pltpu.VMEM((cell_total, 128), bf16),
            pltpu.SemaphoreType.DMA((sources,)),
            pltpu.SemaphoreType.DMA((sources,)),
            pltpu.SemaphoreType.DMA((PIECES + 1,)),
        ],
        compiler_params=pltpu.CompilerParams(
            vmem_limit_bytes=40 * 2**20, collective_id=1, has_side_effects=True
        ),
        name="scatter_geometry",
    )(by_part, feature_grid[0])
    kept, back, stats = pl.pallas_call(
        owner_kernel,
        out_shape=(
            jax.ShapeDtypeStruct((sources, 48, width), bf16),
            jax.ShapeDtypeStruct((4, rows_all, 128), f32),
            jax.ShapeDtypeStruct((sources, 2, 128), f32),
        ),
        in_specs=[pl.BlockSpec(memory_space=pl.ANY), vmem(), pl.BlockSpec(memory_space=pl.ANY)]
        + [vmem()] * 5,
        out_specs=(pl.BlockSpec(memory_space=pl.ANY), vmem(), vmem()),
        scratch_shapes=[
            pltpu.VMEM((sources, 48, width), bf16),
            pltpu.SemaphoreType.DMA((sources,)),
            pltpu.VMEM((cell_total, 128), bf16),
            pltpu.VMEM((2 * cell_total, 128), f32),
            pltpu.VMEM((2 * TILE, 128), f32),
            pltpu.VMEM((2 * TILE, 128), f32),
            pltpu.VMEM((rows_all, 128), f32),
            pltpu.VMEM((rows_all, 128), f32),
            pltpu.VMEM((rows_all, 128), f32),
            pltpu.SMEM((TILE,), jnp.int32),
            pltpu.SMEM((TILE,), jnp.int32),
            pltpu.SemaphoreType.DMA((2,)),
            pltpu.VMEM((TILE // PART * 80, TILE // PART * 32), bf16),
            pltpu.VMEM((fine_mid.shape[1], TILE // PART * 64, TILE // PART * 64), bf16),
            pltpu.VMEM((16, TILE // PART * 64), bf16),
            pltpu.VMEM((16, TILE // PART * 16), bf16),
            pltpu.VMEM((TILE // PART * 32, PART), bf16),
            pltpu.VMEM((TILE // PART * 32, PART), bf16),
        ],
        compiler_params=params,
        name="owner_forward",
    )(
        (sample_cells * 2).reshape(sources * width),
        geometry,
        corners,
        fine_in[0],
        fine_mid[0],
        fine_out,
        prop_in[0],
        prop_out,
    )
    result = pl.pallas_call(
        finish_kernel,
        out_shape=jax.ShapeDtypeStruct((32 + RAY_DEV // 128, 128), f32),
        in_specs=[vmem()] * 5 + [pl.BlockSpec(memory_space=pl.ANY)] * 2,
        out_specs=vmem(),
        scratch_shapes=[
            pltpu.VMEM((sources, 2, 128), f32),
            pltpu.VMEM((sources, 1, 128), f32),
            pltpu.VMEM((sources, 1, 128), f32),
            pltpu.VMEM((lax.axis_size("rep"), 32, 128), f32),
            pltpu.VMEM((sources, 128), f32),
            pltpu.VMEM((slots, slots), bf16),
            pltpu.VMEM((rows_all, 128), f32),
            pltpu.VMEM((32, width), bf16),
            pltpu.VMEM((4, rows_all, 128), f32),
            pltpu.VMEM((sources, 48, width), bf16),
            pltpu.SemaphoreType.DMA((sources,)),
            pltpu.SemaphoreType.DMA((sources,)),
            pltpu.SemaphoreType.DMA((sources,)),
            pltpu.SemaphoreType.DMA((sources,)),
            pltpu.SemaphoreType.DMA((lax.axis_size("rep"),)),
            pltpu.SemaphoreType.DMA((lax.axis_size("rep"),)),
            pltpu.SemaphoreType.DMA((4,)),
        ],
        compiler_params=pltpu.CompilerParams(
            vmem_limit_bytes=58 * 2**20, collective_id=0, has_side_effects=True
        ),
        name="finish",
    )(
        stats,
        slot_ray[0, 0],
        slot_rank[0, 0],
        bucket_count[0],
        prop_out[0].astype(f32)[:, None],
        back,
        kept,
    )
    return (result[32:].reshape(1, 1, RAY_DEV), result[None, 0:16, 0:32], result[16:17, 32:48])


def solution(mesh):
    return jax.shard_map(
        on_device,
        mesh=mesh,
        in_specs=(
            P("dom", None, None),
            P("dom", None, None),
            P("dom", None, None, None),
            P("dom", None),
            P("dom", None, None),
            P("dom", None),
            P("dom", "rep", None, None),
            P(None, "dom", "rep", None, None),
            P("dom", "rep", None, None),
            P("dom", "rep", None, None),
            P("dom", "rep", None),
        ),
        out_specs=(P("dom", "rep", None), P("dom", None, None), P("dom", None)),
        check_vma=False,
    )
```

```python
import functools

import jax
import jax.numpy as jnp
from jax import lax
from jax.experimental import pallas as pl
from jax.experimental.pallas import tpu as pltpu
from jax.sharding import PartitionSpec as P

GR = 32
RAY_DEV = 256
TILE = 1024
PIECES = 4
PART = 256
SHARES = (0, 128, 384, 640, 896, 1024)

distill_weight = 50.0
f32 = jnp.float32
bf16 = jnp.bfloat16
LANES_BOTH = (((1,), (1,)), ((), ()))
MESH = pl.DeviceIdType.MESH


def softplus(x):
    return jnp.maximum(x, 0.0) + jnp.log1p(jnp.exp(-jnp.abs(x)))


def group_total(x):
    once = x + pltpu.roll(x, 32, 1)
    return once + pltpu.roll(once, 64, 1)


def scan_segment(x, rows, forward):
    lane = lax.broadcasted_iota(jnp.int32, x.shape, 1)
    row = lax.broadcasted_iota(jnp.int32, x.shape, 0) % rows
    height = x.shape[0]

    def moved(value, step, axis):
        size = height if axis == 0 else 128
        return pltpu.roll(value, step if forward else size - step, axis)

    within = x
    for step in (32, 64):
        keep = lane >= step if forward else lane < 128 - step
        within = within + jnp.where(keep, moved(within, step, 1), 0.0)
    total = group_total(x)
    running = total
    step = 1
    while step < rows:
        keep = row >= step if forward else row < rows - step
        running = running + jnp.where(keep, moved(running, step, 0), 0.0)
        step *= 2
    edge = row >= 1 if forward else row < rows - 1
    return within + jnp.where(edge, moved(running, 1, 0), 0.0), total


def scatter_kernel(geom_ref, grid_ref, geo_ref, table_hbm, arrived, table, send, recv, local):
    sources = geom_ref.shape[0]
    cell_blocks = grid_ref.shape[1] // 128
    me, replica = lax.axis_index("dom"), lax.axis_index("rep")
    barrier = pltpu.get_barrier_semaphore()

    def greet(step, carry):
        peer = lax.rem(me + step, sources)
        pl.semaphore_signal(barrier, inc=1, device_id=(peer, replica), device_id_type=MESH)
        return carry

    lax.fori_loop(1, sources, greet, 0)

    def copy(step):
        peer = lax.rem(me + step, sources)
        return pltpu.make_async_remote_copy(
            src_ref=geom_ref.at[peer],
            dst_ref=arrived.at[me],
            send_sem=send.at[step],
            recv_sem=recv.at[step],
            device_id=(peer, replica),
            device_id_type=MESH,
        )

    def start(step, carry):
        copy(step).start()
        return carry

    def finish(step, carry):
        copy(step).wait()
        return carry

    own = pltpu.make_async_copy(geom_ref.at[me], arrived.at[me], local.at[PIECES])
    own.start()

    lane = lax.broadcasted_iota(jnp.int32, (GR, 128), 1)
    shifts = (1, GR, GR + 1)

    def block_of(block):
        here = grid_ref[:, pl.ds(pl.multiple_of(block * 128, 128), 128)].astype(f32)
        return (here,) + tuple(pltpu.roll(here, 128 - shift, 1) for shift in shifts)

    def build(block, here):
        there = block_of(jnp.minimum(block + 1, cell_blocks - 1))
        pieces = [here[0]]
        for index, shift in enumerate(shifts):
            pieces.append(jnp.where(lane < 128 - shift, here[index + 1], there[index + 1]))
        table[pl.ds(pl.multiple_of(block * 128, 128), 128), :] = jnp.transpose(
            jnp.concatenate(pieces, axis=0).astype(bf16)
        )
        return there

    state = block_of(0)
    per_piece = cell_blocks // PIECES
    for piece in range(PIECES):
        state = lax.fori_loop(
            piece * per_piece, (piece + 1) * per_piece, build, state, unroll=4
        )
        table_piece(table, table_hbm, local, piece).start()
        if piece == 0:
            pl.semaphore_wait(barrier, sources - 1)
            lax.fori_loop(1, sources, start, 0)
    own.wait()
    lax.fori_loop(1, sources, finish, 0)
    geo_ref[...] = arrived[...].astype(f32)
    for piece in range(PIECES):
        table_piece(table, table_hbm, local, piece).wait()


def table_piece(source, target, sems, piece):
    height = source.shape[0] // PIECES
    rows = pl.ds(piece * height, height)
    return pltpu.make_async_copy(source.at[rows], target.at[rows], sems.at[piece])


def owner_kernel(
    cells_ref, geo, table_hbm, fine_in_ref, fine_mid_ref, fine_out_ref, prop_in_ref, prop_out_ref,
    kept_hbm, back_ref, stats_ref,
    kept_ref, kept_sems, narrow, table, even, odd, fine_logit, prop_logit, spacing, even_cells, odd_cells, sems,
    first_all, mid_all, fine_head, prop_head, even_hold, odd_hold,
):
    sources, rows_kept, width = kept_ref.shape
    tiles_per = width // TILE
    tile_total = sources * tiles_per
    rows_per = width // 128
    for piece in range(PIECES):
        table_piece(table_hbm, narrow, kept_sems, piece).start()

    hidden = fine_in_ref.shape[1]
    groups = TILE // PART

    def diagonal(weights):
        rows, columns = weights.shape
        wide = jnp.concatenate([weights.astype(f32)] * groups, axis=1)
        tall = jnp.concatenate([wide] * groups, axis=0)
        row = lax.broadcasted_iota(jnp.int32, tall.shape, 0) // rows
        column = lax.broadcasted_iota(jnp.int32, tall.shape, 1) // columns
        return jnp.where(row == column, tall, 0.0)

    def heads(weights):
        columns = weights.shape[1]
        wide = jnp.concatenate([weights.astype(f32)] * groups, axis=1)
        tall = jnp.broadcast_to(wide, (16, wide.shape[1]))
        row = lax.broadcasted_iota(jnp.int32, tall.shape, 0)
        column = lax.broadcasted_iota(jnp.int32, tall.shape, 1) // columns
        return jnp.where(row == column, tall, 0.0).astype(bf16)

    first_all[pl.ds(0, groups * hidden), :] = diagonal(
        jnp.transpose(fine_in_ref[...].astype(f32))
    ).astype(bf16)
    first_all[pl.ds(groups * hidden, groups * 16), :] = diagonal(prop_in_ref[...]).astype(bf16)
    for layer in range(fine_mid_ref.shape[0]):
        mid_all[layer] = diagonal(fine_mid_ref[layer]).astype(bf16)
    fine_head[...] = heads(fine_out_ref[...])
    prop_head[...] = heads(prop_out_ref[...])
    eye = (
        lax.broadcasted_iota(jnp.int32, (256, 256), 0)
        == lax.broadcasted_iota(jnp.int32, (256, 256), 1)
    ).astype(f32).astype(bf16)

    cell_blocks = table_hbm.shape[0] // 128
    slab = GR * GR // 128
    per_piece = cell_blocks // PIECES

    def widen(second, block, carry):
        rows = narrow[pl.ds(pl.multiple_of(block * 128, 128), 128), :].astype(f32)
        table[pl.ds(pl.multiple_of(block * 256, 256), 128, stride=2), :] = rows
        if second:
            earlier = pl.multiple_of((block - slab) * 256, 256)
            table[pl.ds(earlier + 1, 128, stride=2), :] = rows
        return carry

    for piece in range(PIECES):
        table_piece(table_hbm, narrow, kept_sems, piece).wait()
        low = piece * per_piece
        if piece == 0:
            lax.fori_loop(0, slab, functools.partial(widen, False), 0)
            low = slab
        lax.fori_loop(low, (piece + 1) * per_piece, functools.partial(widen, True), 0, unroll=4)

    def save(source):
        return pltpu.make_async_copy(
            kept_ref.at[source], kept_hbm.at[source], kept_sems.at[source]
        )

    def fetch(tile, indices, sem):
        start = pl.multiple_of(jnp.minimum(tile, tile_total - 1) * TILE, TILE)
        return pltpu.make_async_copy(cells_ref.at[pl.ds(start, TILE)], indices, sem)

    def gather(indices, low, start=0, stop=TILE):
        for j in range(start, stop):
            cell = pl.multiple_of(indices[j], 2)
            low[pl.ds(2 * j, 2), :] = table[pl.ds(cell, 2), :]

    def interpolate(tile, low, hold):
        source = tile // tiles_per
        first_lane = (tile % tiles_per) * TILE
        places = [
            pl.ds(pl.multiple_of(first_lane + part * PART, PART), PART) for part in range(groups)
        ]
        waiting = []
        for part in range(groups + 1):
            if part < groups:
                start = 2 * part * PART
                rows = jnp.concatenate(
                    [
                        low[pl.ds(start, PART, stride=2), :],
                        low[pl.ds(start + 1, PART, stride=2), :],
                    ],
                    axis=1,
                ).astype(bf16)
                waiting.append(
                    lax.dot_general(eye, rows, LANES_BOTH, preferred_element_type=f32)
                )
            if part > 0:
                lanes = places[part - 1]
                turned = waiting[part - 1]
                place = tile % tiles_per * (TILE // 128) + (part - 1) * (PART // 128)
                offsets = [
                    jnp.concatenate(
                        [
                            geo[source, pl.ds(axis * rows_per + place + piece, 1), :]
                            for piece in range(PART // 128)
                        ],
                        axis=1,
                    )
                    for axis in range(3)
                ]
                factors = [[1.0 - value, value] for value in offsets]
                summed = jnp.zeros((32, PART), f32)
                for corner in range(8):
                    factor = (
                        factors[0][corner // 4]
                        * factors[1][corner // 2 % 2]
                        * factors[2][corner % 2]
                    )
                    summed = summed + turned[corner * 32 : (corner + 1) * 32] * factor
                features = summed.astype(bf16)
                kept_ref[source, pl.ds(0, 32), lanes] = features
                hold[pl.ds((part - 1) * 32, 32), :] = features
            yield

    def networks(tile, hold):
        source = tile // tiles_per
        first_lane = (tile % tiles_per) * TILE
        places = [
            pl.ds(pl.multiple_of(first_lane + part * PART, PART), PART) for part in range(groups)
        ]
        both = jnp.maximum(
            jnp.dot(first_all[...], hold[...], preferred_element_type=f32), 0.0
        ).astype(bf16)
        fine_hidden = both[: groups * hidden]
        prop_hidden = both[groups * hidden :]
        for part in range(groups):
            kept_ref[source, pl.ds(32, 16), places[part]] = prop_hidden[
                part * 16 : (part + 1) * 16
            ]
        yield
        for layer in range(fine_mid_ref.shape[0]):
            fine_hidden = jnp.maximum(
                jnp.dot(mid_all[layer], fine_hidden, preferred_element_type=f32), 0.0
            ).astype(bf16)
            yield
        spacing[pl.ds(pl.multiple_of(tile * (TILE // 128), 8), TILE // 128), :] = geo[
            source,
            pl.ds(
                pl.multiple_of(3 * rows_per + tile % tiles_per * (TILE // 128), 8), TILE // 128
            ),
            :,
        ]
        fine = jnp.dot(fine_head[...], fine_hidden, preferred_element_type=f32)
        prop = jnp.dot(prop_head[...], prop_hidden, preferred_element_type=f32)
        for part in range(groups):
            for piece in range(PART // 128):
                row = pl.ds(tile * (TILE // 128) + (part * PART) // 128 + piece, 1)
                cut = slice(piece * 128, (piece + 1) * 128)
                fine_logit[row, :] = fine[part : part + 1, cut]
                prop_logit[row, :] = prop[part : part + 1, cut]
        yield

    def weave(indices, into, tile, out_of, hold_now, hold_last):
        slots = groups + 1
        ahead = networks(jnp.maximum(tile - 1, 0), hold_last)
        now = interpolate(tile, out_of, hold_now)
        for slot in range(slots):
            gather(indices, into, SHARES[slot], SHARES[slot + 1])
            next(ahead, None)
            next(now, None)
        for unused in ahead:
            pass

    fetch(0, even_cells, sems.at[0]).start()
    fetch(1, odd_cells, sems.at[1]).start()
    fetch(0, even_cells, sems.at[0]).wait()
    gather(even_cells, even)

    def step(tile, carry):
        @pl.when((tile % 2 == 0) & (tile >= 4))
        def _():
            save(tile // 2 - 2).start()

        @pl.when(tile % 2 == 0)
        def _():
            fetch(tile + 2, even_cells, sems.at[0]).start()
            fetch(tile + 1, odd_cells, sems.at[1]).wait()
            weave(odd_cells, odd, tile, even, even_hold, odd_hold)

        @pl.when(tile % 2 == 1)
        def _():
            fetch(tile + 2, odd_cells, sems.at[1]).start()
            fetch(tile + 1, even_cells, sems.at[0]).wait()
            weave(even_cells, even, tile, odd, odd_hold, even_hold)

        return carry

    lax.fori_loop(0, tile_total, step, 0)
    fetch(tile_total, odd_cells, sems.at[1]).wait()
    for unused in networks(tile_total - 1, odd_hold):
        pass

    save(sources - 2).start()
    save(sources - 1).start()

    gap = spacing[...]
    prop_raw = prop_logit[...]
    optical = softplus(prop_raw) * gap
    depth, prop_total = scan_segment(optical, rows_per, True)
    before = jnp.exp(optical - depth)
    prop_taken = before - jnp.exp(-depth)
    back_ref[0] = prop_taken
    back_ref[1] = before
    back_ref[2] = gap * jax.nn.sigmoid(prop_raw)
    fine_optical = softplus(fine_logit[...]) * gap
    fine_depth, fine_total = scan_segment(fine_optical, rows_per, True)
    fine_taken = jnp.exp(fine_optical - fine_depth) - jnp.exp(-fine_depth)
    back_ref[3] = fine_taken

    def per_segment(value, totalled):
        over_rows = jnp.sum(value.reshape(sources, rows_per, 128), axis=1)
        return over_rows if totalled else group_total(over_rows)

    sum_aa = per_segment(prop_taken * prop_taken, False)
    sum_ab = per_segment(prop_taken * fine_taken, False)
    sum_bb = per_segment(fine_taken * fine_taken, False)
    log_prop = -per_segment(prop_total, True)
    log_fine = -per_segment(fine_total, True)
    part = lax.broadcasted_iota(jnp.int32, (sources, 128), 1) // 32
    stats_ref[:, 0, :] = jnp.where(
        part == 0, sum_aa, jnp.where(part == 1, sum_ab, jnp.where(part == 2, sum_bb, log_prop))
    )
    stats_ref[:, 1, :] = log_fine

    def saved(source, carry):
        save(source).wait()
        return carry

    lax.fori_loop(0, sources, saved, 0)


def split_three(value):
    high = value.astype(bf16)
    rest = value - high.astype(f32)
    middle = rest.astype(bf16)
    low = (rest - middle.astype(f32)).astype(bf16)
    return [high, middle, low]


def finish_kernel(
    stats_ref, ray_ref, rank_ref, count_ref, prop_out_ref, back_hbm, kept_hbm,
    result_ref,
    stats_in, factors_out, factors_in, grads_in, flat, ahead, logit_grad, left, back_ref, kept_ref,
    stats_send, stats_recv, factors_send, factors_recv, grads_send, grads_recv, local,
):
    sources, rows_kept, width = kept_ref.shape
    rows_per = width // 128
    slots = ahead.shape[0]
    blocks = slots // 128
    me, replica = lax.axis_index("dom"), lax.axis_index("rep")
    replicas = lax.axis_size("rep")

    load_kept = pltpu.make_async_copy(kept_hbm, kept_ref, local.at[0])
    load_back = pltpu.make_async_copy(back_hbm, back_ref, local.at[1])
    load_back.start()
    load_kept.start()

    barrier = pltpu.get_barrier_semaphore()

    def greet(step, carry):
        peer = lax.rem(me + step, sources)
        pl.semaphore_signal(barrier, inc=1, device_id=(peer, replica), device_id_type=MESH)
        return carry

    lax.fori_loop(1, sources, greet, 0)
    for step in range(1, replicas):
        other = lax.rem(replica + step, replicas)
        pl.semaphore_signal(barrier, inc=1, device_id=(me, other), device_id_type=MESH)

    def exchange(source, target, send, recv):
        def copy(step):
            peer = lax.rem(me + step, sources)
            return pltpu.make_async_remote_copy(
                src_ref=source.at[peer],
                dst_ref=target.at[me],
                send_sem=send.at[step],
                recv_sem=recv.at[step],
                device_id=(peer, replica),
                device_id_type=MESH,
            )

        def start(step, carry):
            copy(step).start()
            return carry

        def finish(step, carry):
            copy(step).wait()
            return carry

        lax.fori_loop(1, sources, start, 0)
        return lambda: lax.fori_loop(1, sources, finish, 0)


    part_row = lax.broadcasted_iota(jnp.int32, (sources, 128), 0)
    group = lax.broadcasted_iota(jnp.int32, (sources, 128), 1) // 32
    seat = part_row % 4
    fold = jnp.where(
        lax.broadcasted_iota(jnp.int32, (blocks, sources), 0)
        == lax.broadcasted_iota(jnp.int32, (blocks, sources), 1) // 4,
        1.0,
        0.0,
    )
    unfold = jnp.where(
        lax.broadcasted_iota(jnp.int32, (sources, blocks), 0) // 4
        == lax.broadcasted_iota(jnp.int32, (sources, blocks), 1),
        1.0,
        0.0,
    )

    def exact(first, second):
        return jnp.dot(first, second, precision=lax.Precision.HIGHEST, preferred_element_type=f32)

    def dense(*seated):
        masked = [jnp.where(group == seat, value, 0.0) for value in seated]
        folded = exact(fold, jnp.concatenate(masked, axis=1))
        return [folded[:, i * 128 : (i + 1) * 128] for i in range(len(seated))]

    def four(value):
        return jnp.concatenate([value] * 4, axis=1)

    def as_row(value):
        return jnp.concatenate([value[b : b + 1] for b in range(blocks)], axis=1)

    def as_dense(value):
        return jnp.concatenate(
            [value[:, b * 128 : (b + 1) * 128] for b in range(blocks)], axis=0
        )

    counts = jnp.broadcast_to(count_ref[...].astype(f32), (sources, sources))
    diagonal = lax.broadcasted_iota(jnp.int32, (sources, sources), 0) == lax.broadcasted_iota(
        jnp.int32, (sources, sources), 1
    )
    count_column = jnp.sum(jnp.where(diagonal, counts, 0.0), axis=1, keepdims=True)
    slot_lane = (lax.broadcasted_iota(jnp.int32, (sources, 128), 1) % 32).astype(f32)
    live, rays, ranks = dense(
        jnp.where(slot_lane < count_column, 1.0, 0.0),
        four(ray_ref[...].astype(f32)),
        four(rank_ref[...].astype(f32)),
    )
    live = as_row(live)
    keys = rays * 64.0 + ranks
    key_row, rank_row = as_row(keys), as_row(ranks)
    key_column, ray_column = jnp.transpose(keys), jnp.transpose(rays)
    pl.semaphore_wait(barrier, sources + replicas - 2)
    wait_stats = exchange(stats_ref, stats_in, stats_send, stats_recv)
    own_stats = pltpu.make_async_copy(stats_ref.at[me], stats_in.at[me], local.at[2])
    own_stats.start()

    for chunk in range(blocks):
        gap = key_row - key_column[:, chunk : chunk + 1]
        ahead[pl.ds(chunk * 128, 128), :] = jnp.where(
            (gap > 0.5) & (gap < rank_row + 0.5), 1.0, 0.0
        ).astype(bf16)

    own_stats.wait()
    wait_stats()

    for index in range(sources):
        flat[pl.ds(index, 1), :] = stats_in[index, pl.ds(0, 1), :]
    packed = flat[...]
    turned = [packed] + [pltpu.roll(packed, 32 * step, 1) for step in range(1, 4)]

    def stat(index):
        value = turned[(3 - index) % 4]
        for place in range(3):
            value = jnp.where(seat == place, turned[(place - index) % 4], value)
        return value

    for index in range(sources):
        flat[pl.ds(index, 1), :] = stats_in[index, pl.ds(1, 1), :]
    sum_aa, sum_ab, sum_bb, log_prop, log_fine = (
        as_row(value) for value in dense(*(stat(index) for index in range(4)), flat[...])
    )

    def stacked(values):
        pieces = [piece.astype(f32) for value in values for piece in split_three(value)]
        pieces += [jnp.zeros_like(pieces[0])] * (8 - len(pieces))
        return jnp.concatenate(pieces, axis=0).astype(bf16)

    logs = stacked([log_prop * live, log_fine * live])
    reached = jnp.dot(logs, ahead[...], preferred_element_type=f32)
    entry_prop = jnp.exp(reached[0:1] + reached[1:2] + reached[2:3]) * live
    entry_fine = jnp.exp(reached[3:4] + reached[4:5] + reached[5:6]) * live
    slot_grad = distill_weight * (entry_prop * sum_aa - entry_fine * sum_ab) * entry_prop
    carried = lax.dot_general(
        stacked([slot_grad]), ahead[...], LANES_BOTH, preferred_element_type=f32
    )
    outgoing = (
        0.5 * distill_weight * entry_prop * entry_prop,
        -distill_weight * entry_prop * entry_fine,
        (carried[0:1] + carried[1:2] + carried[2:3]) * live,
    )
    message = jnp.zeros((sources, 128), f32)
    spreads = exact(unfold, jnp.concatenate([as_dense(value) for value in outgoing], axis=1))
    for index in range(len(outgoing)):
        spread = spreads[:, index * 128 : (index + 1) * 128]
        for place in range(4):
            shift = 32 * ((index - place) % 4)
            moved = pltpu.roll(spread, shift, 1) if shift else spread
            message = jnp.where((group == index) & (seat == place), moved, message)
    for index in range(sources):
        factors_out[index] = message[index : index + 1]

    wait_factors = exchange(factors_out, factors_in, factors_send, factors_recv)
    own_factors = pltpu.make_async_copy(factors_out.at[me], factors_in.at[me], local.at[3])
    own_factors.start()

    seg_loss = (
        entry_prop * entry_prop * sum_aa
        - 2.0 * entry_prop * entry_fine * sum_ab
        + entry_fine * entry_fine * sum_bb
    )
    losses = stacked([seg_loss])
    ray_loss = jnp.zeros((8, RAY_DEV), f32)
    ray_ids = lax.broadcasted_iota(jnp.int32, (128, RAY_DEV), 1).astype(f32)
    for chunk in range(blocks):
        mask = jnp.where(ray_column[:, chunk : chunk + 1] == ray_ids, 1.0, 0.0).astype(bf16)
        ray_loss = ray_loss + jnp.dot(
            losses[:, chunk * 128 : (chunk + 1) * 128], mask, preferred_element_type=f32
        )
    ray_loss = 0.5 * distill_weight * (ray_loss[0:1] + ray_loss[1:2] + ray_loss[2:3])
    for index in range(RAY_DEV // 128):
        result_ref[pl.ds(32 + index, 1), :] = ray_loss[:, index * 128 : (index + 1) * 128]

    load_back.wait()
    load_kept.wait()
    own_factors.wait()
    wait_factors()

    for index in range(sources):
        flat[pl.ds(index, 1), :] = factors_in[index]
    factors = flat[...]

    def to_samples(index):
        spread = group_total(jnp.where(group == index, factors, 0.0))
        return jnp.broadcast_to(spread[:, None, :], (sources, rows_per, 128)).reshape(
            sources * rows_per, 128
        )

    taken = back_ref[0]
    taken_grad = 2.0 * to_samples(0) * taken + to_samples(1) * back_ref[3]
    behind, unused = scan_segment(taken_grad * taken, rows_per, False)
    grad = (taken_grad * back_ref[1] - behind - to_samples(2)) * back_ref[2]
    logit_grad[...] = grad.astype(bf16).astype(f32)

    def accumulate(source, total):
        for part_index in range(rows_per):
            lanes = pl.ds(part_index * 128, 128)
            row = logit_grad[pl.ds(source * rows_per + part_index, 1), :]
            hidden = kept_ref[source, pl.ds(32, 16), lanes].astype(f32)
            wide = jnp.broadcast_to(row, (16, 128))
            left[pl.ds(0, 16), lanes] = jnp.where(hidden > 0, wide, 0.0).astype(bf16)
            left[pl.ds(16, 16), lanes] = wide.astype(bf16)
        return total + lax.dot_general(
            left[...], kept_ref[source], LANES_BOTH, preferred_element_type=f32
        )

    total = lax.fori_loop(0, sources, accumulate, jnp.zeros((32, rows_kept), f32))
    grads_in[replica] = jnp.concatenate([total, jnp.zeros((32, 128 - rows_kept), f32)], axis=1)

    def share(step):
        other = lax.rem(replica + step, replicas)
        return pltpu.make_async_remote_copy(
            src_ref=grads_in.at[replica],
            dst_ref=grads_in.at[replica],
            send_sem=grads_send.at[step],
            recv_sem=grads_recv.at[step],
            device_id=(me, other),
            device_id_type=MESH,
        )

    for step in range(1, replicas):
        share(step).start()
    for step in range(1, replicas):
        share(step).wait()
    summed = grads_in[0]
    for index in range(1, replicas):
        summed = summed + grads_in[index]
    head = jnp.broadcast_to(prop_out_ref[...].astype(f32), (16, 16))
    on_diagonal = lax.broadcasted_iota(jnp.int32, (16, 16), 0) == lax.broadcasted_iota(
        jnp.int32, (16, 16), 1
    )
    head_column = jnp.sum(jnp.where(on_diagonal, head, 0.0), axis=1, keepdims=True)
    result_ref[pl.ds(0, 16), :] = summed[0:16] * head_column
    result_ref[pl.ds(16, 16), :] = summed[16:32]


def split_kernel(result_ref, loss_ref, in_ref, out_ref):
    loss_ref[...] = result_ref[pl.ds(32, RAY_DEV // 128), :]
    in_ref[...] = result_ref[pl.ds(0, 16), :][:, 0:32]
    out_ref[...] = result_ref[pl.ds(16, 1), :][:, 32:48]


def vmem():
    return pl.BlockSpec(memory_space=pltpu.VMEM)


def on_device(
    feature_grid,
    fine_in,
    fine_mid,
    fine_out,
    prop_in,
    prop_out,
    sample_cells,
    sample_geometry,
    slot_ray,
    slot_rank,
    bucket_count,
):
    sources = lax.axis_size("dom")
    capacity = slot_ray.shape[3]
    width = sample_cells.shape[3]
    rows_all = sources * width // 128
    slots = sources * capacity
    cell_total = feature_grid.shape[2]
    params = pltpu.CompilerParams(vmem_limit_bytes=60 * 2**20)

    by_part = (
        sample_geometry.reshape(4, sources, width)
        .transpose(1, 0, 2)
        .reshape(sources, 4 * width // 128, 128)
    )
    geometry, corners = pl.pallas_call(
        scatter_kernel,
        out_shape=(
            jax.ShapeDtypeStruct(by_part.shape, f32),
            jax.ShapeDtypeStruct((cell_total, 128), bf16),
        ),
        in_specs=[vmem()] * 2,
        out_specs=(vmem(), pl.BlockSpec(memory_space=pl.ANY)),
        scratch_shapes=[
            pltpu.VMEM(by_part.shape, bf16),
            pltpu.VMEM((cell_total, 128), bf16),
            pltpu.SemaphoreType.DMA((sources,)),
            pltpu.SemaphoreType.DMA((sources,)),
            pltpu.SemaphoreType.DMA((PIECES + 1,)),
        ],
        compiler_params=pltpu.CompilerParams(
            vmem_limit_bytes=60 * 2**20, collective_id=1, has_side_effects=True
        ),
        name="scatter_geometry",
    )(by_part, feature_grid[0])
    kept, back, stats = pl.pallas_call(
        owner_kernel,
        out_shape=(
            jax.ShapeDtypeStruct((sources, 48, width), bf16),
            jax.ShapeDtypeStruct((4, rows_all, 128), f32),
            jax.ShapeDtypeStruct((sources, 2, 128), f32),
        ),
        in_specs=[pl.BlockSpec(memory_space=pl.ANY), vmem(), pl.BlockSpec(memory_space=pl.ANY)]
        + [vmem()] * 5,
        out_specs=(pl.BlockSpec(memory_space=pl.ANY), vmem(), vmem()),
        scratch_shapes=[
            pltpu.VMEM((sources, 48, width), bf16),
            pltpu.SemaphoreType.DMA((sources,)),
            pltpu.VMEM((cell_total, 128), bf16),
            pltpu.VMEM((2 * cell_total, 128), f32),
            pltpu.VMEM((2 * TILE, 128), f32),
            pltpu.VMEM((2 * TILE, 128), f32),
            pltpu.VMEM((rows_all, 128), f32),
            pltpu.VMEM((rows_all, 128), f32),
            pltpu.VMEM((rows_all, 128), f32),
            pltpu.SMEM((TILE,), jnp.int32),
            pltpu.SMEM((TILE,), jnp.int32),
            pltpu.SemaphoreType.DMA((2,)),
            pltpu.VMEM((TILE // PART * 80, TILE // PART * 32), bf16),
            pltpu.VMEM((fine_mid.shape[1], TILE // PART * 64, TILE // PART * 64), bf16),
            pltpu.VMEM((16, TILE // PART * 64), bf16),
            pltpu.VMEM((16, TILE // PART * 16), bf16),
            pltpu.VMEM((TILE // PART * 32, PART), bf16),
            pltpu.VMEM((TILE // PART * 32, PART), bf16),
        ],
        compiler_params=params,
        name="owner_forward",
    )(
        (sample_cells * 2).reshape(sources * width),
        geometry,
        corners,
        jnp.swapaxes(fine_in, 1, 2)[0],
        fine_mid[0],
        fine_out,
        prop_in[0],
        prop_out,
    )
    result = pl.pallas_call(
        finish_kernel,
        out_shape=jax.ShapeDtypeStruct((32 + RAY_DEV // 128, 128), f32),
        in_specs=[vmem()] * 5 + [pl.BlockSpec(memory_space=pl.ANY)] * 2,
        out_specs=vmem(),
        scratch_shapes=[
            pltpu.VMEM((sources, 2, 128), f32),
            pltpu.VMEM((sources, 1, 128), f32),
            pltpu.VMEM((sources, 1, 128), f32),
            pltpu.VMEM((lax.axis_size("rep"), 32, 128), f32),
            pltpu.VMEM((sources, 128), f32),
            pltpu.VMEM((slots, slots), bf16),
            pltpu.VMEM((rows_all, 128), f32),
            pltpu.VMEM((32, width), bf16),
            pltpu.VMEM((4, rows_all, 128), f32),
            pltpu.VMEM((sources, 48, width), bf16),
            pltpu.SemaphoreType.DMA((sources,)),
            pltpu.SemaphoreType.DMA((sources,)),
            pltpu.SemaphoreType.DMA((sources,)),
            pltpu.SemaphoreType.DMA((sources,)),
            pltpu.SemaphoreType.DMA((lax.axis_size("rep"),)),
            pltpu.SemaphoreType.DMA((lax.axis_size("rep"),)),
            pltpu.SemaphoreType.DMA((4,)),
        ],
        compiler_params=pltpu.CompilerParams(
            vmem_limit_bytes=58 * 2**20, collective_id=0, has_side_effects=True
        ),
        name="finish",
    )(
        stats,
        slot_ray[0, 0],
        slot_rank[0, 0],
        bucket_count[0],
        prop_out,
        back,
        kept,
    )
    ray_loss, in_grad, out_grad = pl.pallas_call(
        split_kernel,
        out_shape=(
            jax.ShapeDtypeStruct((RAY_DEV // 128, 128), f32),
            jax.ShapeDtypeStruct((16, 32), f32),
            jax.ShapeDtypeStruct((1, 16), f32),
        ),
        in_specs=[vmem()],
        out_specs=(vmem(), vmem(), vmem()),
        name="split",
    )(result)
    return (ray_loss.reshape(1, 1, RAY_DEV), in_grad[None], out_grad)


def solution(mesh):
    return jax.shard_map(
        on_device,
        mesh=mesh,
        in_specs=(
            P("dom", None, None),
            P("dom", None, None),
            P("dom", None, None, None),
            P("dom", None),
            P("dom", None, None),
            P("dom", None),
            P("dom", "rep", None, None),
            P(None, "dom", "rep", None, None),
            P("dom", "rep", None, None),
            P("dom", "rep", None, None),
            P("dom", "rep", None),
        ),
        out_specs=(P("dom", "rep", None), P("dom", None, None), P("dom", None)),
        check_vma=False,
    )
```

```python
import functools

import jax
import jax.numpy as jnp
from jax import lax
from jax.experimental import pallas as pl
from jax.experimental.pallas import tpu as pltpu
from jax.sharding import PartitionSpec as P

GR = 32
RAY_DEV = 256
TILE = 2048
PIECES = 4
PART = 512
SHARES = (0, 256, 768, 1280, 1792, 2048)

distill_weight = 50.0
f32 = jnp.float32
bf16 = jnp.bfloat16
LANES_BOTH = (((1,), (1,)), ((), ()))
MESH = pl.DeviceIdType.MESH


def softplus(x):
    return jnp.maximum(x, 0.0) + jnp.log1p(jnp.exp(-jnp.abs(x)))


def group_total(x):
    once = x + pltpu.roll(x, 32, 1)
    return once + pltpu.roll(once, 64, 1)


def scan_segment(x, rows, forward):
    lane = lax.broadcasted_iota(jnp.int32, x.shape, 1)
    row = lax.broadcasted_iota(jnp.int32, x.shape, 0) % rows
    height = x.shape[0]

    def moved(value, step, axis):
        size = height if axis == 0 else 128
        return pltpu.roll(value, step if forward else size - step, axis)

    within = x
    for step in (32, 64):
        keep = lane >= step if forward else lane < 128 - step
        within = within + jnp.where(keep, moved(within, step, 1), 0.0)
    total = group_total(x)
    running = total
    step = 1
    while step < rows:
        keep = row >= step if forward else row < rows - step
        running = running + jnp.where(keep, moved(running, step, 0), 0.0)
        step *= 2
    edge = row >= 1 if forward else row < rows - 1
    return within + jnp.where(edge, moved(running, 1, 0), 0.0), total


def scatter_kernel(geom_ref, grid_ref, geo_ref, table_hbm, arrived, table, send, recv, local):
    sources = geom_ref.shape[0]
    cell_blocks = grid_ref.shape[1] // 128
    me, replica = lax.axis_index("dom"), lax.axis_index("rep")
    barrier = pltpu.get_barrier_semaphore()

    def greet(step, carry):
        peer = lax.rem(me + step, sources)
        pl.semaphore_signal(barrier, inc=1, device_id=(peer, replica), device_id_type=MESH)
        return carry

    lax.fori_loop(1, sources, greet, 0)

    def copy(step):
        peer = lax.rem(me + step, sources)
        return pltpu.make_async_remote_copy(
            src_ref=geom_ref.at[peer],
            dst_ref=arrived.at[me],
            send_sem=send.at[step],
            recv_sem=recv.at[step],
            device_id=(peer, replica),
            device_id_type=MESH,
        )

    def start(step, carry):
        copy(step).start()
        return carry

    def finish(step, carry):
        copy(step).wait()
        return carry

    own = pltpu.make_async_copy(geom_ref.at[me], arrived.at[me], local.at[PIECES])
    own.start()

    lane = lax.broadcasted_iota(jnp.int32, (GR, 128), 1)
    shifts = (1, GR, GR + 1)

    def block_of(block):
        here = grid_ref[:, pl.ds(pl.multiple_of(block * 128, 128), 128)].astype(f32)
        return (here,) + tuple(pltpu.roll(here, 128 - shift, 1) for shift in shifts)

    def build(block, here):
        there = block_of(jnp.minimum(block + 1, cell_blocks - 1))
        pieces = [here[0]]
        for index, shift in enumerate(shifts):
            pieces.append(jnp.where(lane < 128 - shift, here[index + 1], there[index + 1]))
        table[pl.ds(pl.multiple_of(block * 128, 128), 128), :] = jnp.transpose(
            jnp.concatenate(pieces, axis=0).astype(bf16)
        )
        return there

    state = block_of(0)
    per_piece = cell_blocks // PIECES
    for piece in range(PIECES):
        state = lax.fori_loop(
            piece * per_piece, (piece + 1) * per_piece, build, state, unroll=4
        )
        table_piece(table, table_hbm, local, piece).start()
        if piece == 0:
            pl.semaphore_wait(barrier, sources - 1)
            lax.fori_loop(1, sources, start, 0)
    own.wait()
    lax.fori_loop(1, sources, finish, 0)
    geo_ref[...] = arrived[...].astype(f32)
    for piece in range(PIECES):
        table_piece(table, table_hbm, local, piece).wait()


def table_piece(source, target, sems, piece):
    height = source.shape[0] // PIECES
    rows = pl.ds(piece * height, height)
    return pltpu.make_async_copy(source.at[rows], target.at[rows], sems.at[piece])


def owner_kernel(
    cells_ref, geo, table_hbm, fine_in_ref, fine_mid_ref, fine_out_ref, prop_in_ref, prop_out_ref,
    kept_hbm, back_ref, stats_ref,
    kept_ref, kept_sems, narrow, table, even, odd, fine_logit, prop_logit, spacing, even_cells, odd_cells, sems,
    first_all, mid_all, fine_head, prop_head, even_hold, odd_hold,
):
    sources, rows_kept, width = kept_ref.shape
    tiles_per = width // TILE
    tile_total = sources * tiles_per
    rows_per = width // 128
    for piece in range(PIECES):
        table_piece(table_hbm, narrow, kept_sems, piece).start()

    hidden = fine_in_ref.shape[1]
    groups = TILE // PART

    def diagonal(weights):
        rows, columns = weights.shape
        wide = jnp.concatenate([weights.astype(f32)] * groups, axis=1)
        tall = jnp.concatenate([wide] * groups, axis=0)
        row = lax.broadcasted_iota(jnp.int32, tall.shape, 0) // rows
        column = lax.broadcasted_iota(jnp.int32, tall.shape, 1) // columns
        return jnp.where(row == column, tall, 0.0)

    def heads(weights):
        columns = weights.shape[1]
        wide = jnp.concatenate([weights.astype(f32)] * groups, axis=1)
        tall = jnp.broadcast_to(wide, (16, wide.shape[1]))
        row = lax.broadcasted_iota(jnp.int32, tall.shape, 0)
        column = lax.broadcasted_iota(jnp.int32, tall.shape, 1) // columns
        return jnp.where(row == column, tall, 0.0).astype(bf16)

    first_all[pl.ds(0, groups * hidden), :] = diagonal(
        jnp.transpose(fine_in_ref[...].astype(f32))
    ).astype(bf16)
    first_all[pl.ds(groups * hidden, groups * 16), :] = diagonal(prop_in_ref[...]).astype(bf16)
    for layer in range(fine_mid_ref.shape[0]):
        mid_all[layer] = diagonal(fine_mid_ref[layer]).astype(bf16)
    fine_head[...] = heads(fine_out_ref[...])
    prop_head[...] = heads(prop_out_ref[...])
    eye = (
        lax.broadcasted_iota(jnp.int32, (256, 256), 0)
        == lax.broadcasted_iota(jnp.int32, (256, 256), 1)
    ).astype(f32).astype(bf16)

    cell_blocks = table_hbm.shape[0] // 128
    slab = GR * GR // 128
    per_piece = cell_blocks // PIECES

    def widen(second, block, carry):
        rows = narrow[pl.ds(pl.multiple_of(block * 128, 128), 128), :].astype(f32)
        table[pl.ds(pl.multiple_of(block * 256, 256), 128, stride=2), :] = rows
        if second:
            earlier = pl.multiple_of((block - slab) * 256, 256)
            table[pl.ds(earlier + 1, 128, stride=2), :] = rows
        return carry

    for piece in range(PIECES):
        table_piece(table_hbm, narrow, kept_sems, piece).wait()
        low = piece * per_piece
        if piece == 0:
            lax.fori_loop(0, slab, functools.partial(widen, False), 0)
            low = slab
        lax.fori_loop(low, (piece + 1) * per_piece, functools.partial(widen, True), 0, unroll=4)

    def save(source):
        return pltpu.make_async_copy(
            kept_ref.at[source], kept_hbm.at[source], kept_sems.at[source]
        )

    def fetch(tile, indices, sem):
        start = pl.multiple_of(jnp.minimum(tile, tile_total - 1) * TILE, TILE)
        return pltpu.make_async_copy(cells_ref.at[pl.ds(start, TILE)], indices, sem)

    def gather(indices, low, start=0, stop=TILE):
        for j in range(start, stop):
            cell = pl.multiple_of(indices[j], 2)
            low[pl.ds(2 * j, 2), :] = table[pl.ds(cell, 2), :]

    def interpolate(tile, low, hold):
        source = tile // tiles_per
        first_lane = (tile % tiles_per) * TILE
        places = [
            pl.ds(pl.multiple_of(first_lane + part * PART, PART), PART) for part in range(groups)
        ]
        waiting = []
        for part in range(groups + 1):
            if part < groups:
                start = 2 * part * PART
                rows = jnp.concatenate(
                    [
                        low[pl.ds(start, PART, stride=2), :],
                        low[pl.ds(start + 1, PART, stride=2), :],
                    ],
                    axis=1,
                ).astype(bf16)
                waiting.append(
                    lax.dot_general(eye, rows, LANES_BOTH, preferred_element_type=f32)
                )
            if part > 0:
                lanes = places[part - 1]
                turned = waiting[part - 1]
                place = tile % tiles_per * (TILE // 128) + (part - 1) * (PART // 128)
                offsets = [
                    jnp.concatenate(
                        [
                            geo[source, pl.ds(axis * rows_per + place + piece, 1), :]
                            for piece in range(PART // 128)
                        ],
                        axis=1,
                    )
                    for axis in range(3)
                ]
                factors = [[1.0 - value, value] for value in offsets]
                summed = jnp.zeros((32, PART), f32)
                for corner in range(8):
                    factor = (
                        factors[0][corner // 4]
                        * factors[1][corner // 2 % 2]
                        * factors[2][corner % 2]
                    )
                    summed = summed + turned[corner * 32 : (corner + 1) * 32] * factor
                features = summed.astype(bf16)
                kept_ref[source, pl.ds(0, 32), lanes] = features
                hold[pl.ds((part - 1) * 32, 32), :] = features
            yield

    def networks(tile, hold):
        source = tile // tiles_per
        first_lane = (tile % tiles_per) * TILE
        places = [
            pl.ds(pl.multiple_of(first_lane + part * PART, PART), PART) for part in range(groups)
        ]
        both = jnp.maximum(
            jnp.dot(first_all[...], hold[...], preferred_element_type=f32), 0.0
        ).astype(bf16)
        fine_hidden = both[: groups * hidden]
        prop_hidden = both[groups * hidden :]
        for part in range(groups):
            kept_ref[source, pl.ds(32, 16), places[part]] = prop_hidden[
                part * 16 : (part + 1) * 16
            ]
        yield
        for layer in range(fine_mid_ref.shape[0]):
            fine_hidden = jnp.maximum(
                jnp.dot(mid_all[layer], fine_hidden, preferred_element_type=f32), 0.0
            ).astype(bf16)
            yield
        spacing[pl.ds(pl.multiple_of(tile * (TILE // 128), 8), TILE // 128), :] = geo[
            source,
            pl.ds(
                pl.multiple_of(3 * rows_per + tile % tiles_per * (TILE // 128), 8), TILE // 128
            ),
            :,
        ]
        fine = jnp.dot(fine_head[...], fine_hidden, preferred_element_type=f32)
        prop = jnp.dot(prop_head[...], prop_hidden, preferred_element_type=f32)
        for part in range(groups):
            for piece in range(PART // 128):
                row = pl.ds(tile * (TILE // 128) + (part * PART) // 128 + piece, 1)
                cut = slice(piece * 128, (piece + 1) * 128)
                fine_logit[row, :] = fine[part : part + 1, cut]
                prop_logit[row, :] = prop[part : part + 1, cut]
        yield

    def weave(indices, into, tile, out_of, hold_now, hold_last):
        slots = groups + 1
        ahead = networks(jnp.maximum(tile - 1, 0), hold_last)
        now = interpolate(tile, out_of, hold_now)
        for slot in range(slots):
            next(now, None)
            gather(indices, into, SHARES[slot], SHARES[slot + 1])
            next(ahead, None)
        for unused in ahead:
            pass

    fetch(0, even_cells, sems.at[0]).start()
    fetch(1, odd_cells, sems.at[1]).start()
    fetch(0, even_cells, sems.at[0]).wait()
    gather(even_cells, even)

    def step(tile, carry):
        @pl.when(tile >= 2)
        def _():
            save(tile - 2).start()

        @pl.when(tile % 2 == 0)
        def _():
            fetch(tile + 2, even_cells, sems.at[0]).start()
            fetch(tile + 1, odd_cells, sems.at[1]).wait()
            weave(odd_cells, odd, tile, even, even_hold, odd_hold)

        @pl.when(tile % 2 == 1)
        def _():
            fetch(tile + 2, odd_cells, sems.at[1]).start()
            fetch(tile + 1, even_cells, sems.at[0]).wait()
            weave(even_cells, even, tile, odd, odd_hold, even_hold)

        return carry

    lax.fori_loop(0, tile_total, step, 0)
    fetch(tile_total, odd_cells, sems.at[1]).wait()
    for unused in networks(tile_total - 1, odd_hold):
        pass

    save(sources - 2).start()
    save(sources - 1).start()

    gap = spacing[...]
    prop_raw = prop_logit[...]
    optical = softplus(prop_raw) * gap
    depth, prop_total = scan_segment(optical, rows_per, True)
    before = jnp.exp(optical - depth)
    prop_taken = before - jnp.exp(-depth)
    back_ref[0] = prop_taken
    back_ref[1] = before
    back_ref[2] = gap * jax.nn.sigmoid(prop_raw)
    fine_optical = softplus(fine_logit[...]) * gap
    fine_depth, fine_total = scan_segment(fine_optical, rows_per, True)
    fine_taken = jnp.exp(fine_optical - fine_depth) - jnp.exp(-fine_depth)
    back_ref[3] = fine_taken

    def per_segment(value, totalled):
        over_rows = jnp.sum(value.reshape(sources, rows_per, 128), axis=1)
        return over_rows if totalled else group_total(over_rows)

    sum_aa = per_segment(prop_taken * prop_taken, False)
    sum_ab = per_segment(prop_taken * fine_taken, False)
    sum_bb = per_segment(fine_taken * fine_taken, False)
    log_prop = -per_segment(prop_total, True)
    log_fine = -per_segment(fine_total, True)
    part = lax.broadcasted_iota(jnp.int32, (sources, 128), 1) // 32
    stats_ref[:, 0, :] = jnp.where(
        part == 0, sum_aa, jnp.where(part == 1, sum_ab, jnp.where(part == 2, sum_bb, log_prop))
    )
    stats_ref[:, 1, :] = log_fine

    def saved(source, carry):
        save(source).wait()
        return carry

    lax.fori_loop(0, sources, saved, 0)


def split_three(value):
    high = value.astype(bf16)
    rest = value - high.astype(f32)
    middle = rest.astype(bf16)
    low = (rest - middle.astype(f32)).astype(bf16)
    return [high, middle, low]


def finish_kernel(
    stats_ref, ray_ref, rank_ref, count_ref, prop_out_ref, back_hbm, kept_hbm,
    result_ref,
    stats_in, factors_out, factors_in, grads_in, flat, ahead, logit_grad, left, back_ref, kept_ref,
    stats_send, stats_recv, factors_send, factors_recv, grads_send, grads_recv, local,
):
    sources, rows_kept, width = kept_ref.shape
    rows_per = width // 128
    slots = ahead.shape[0]
    blocks = slots // 128
    me, replica = lax.axis_index("dom"), lax.axis_index("rep")
    replicas = lax.axis_size("rep")

    load_kept = pltpu.make_async_copy(kept_hbm, kept_ref, local.at[0])
    load_back = pltpu.make_async_copy(back_hbm, back_ref, local.at[1])
    load_back.start()
    load_kept.start()

    barrier = pltpu.get_barrier_semaphore()

    def greet(step, carry):
        peer = lax.rem(me + step, sources)
        pl.semaphore_signal(barrier, inc=1, device_id=(peer, replica), device_id_type=MESH)
        return carry

    lax.fori_loop(1, sources, greet, 0)
    for step in range(1, replicas):
        other = lax.rem(replica + step, replicas)
        pl.semaphore_signal(barrier, inc=1, device_id=(me, other), device_id_type=MESH)

    def exchange(source, target, send, recv):
        def copy(step):
            peer = lax.rem(me + step, sources)
            return pltpu.make_async_remote_copy(
                src_ref=source.at[peer],
                dst_ref=target.at[me],
                send_sem=send.at[step],
                recv_sem=recv.at[step],
                device_id=(peer, replica),
                device_id_type=MESH,
            )

        def start(step, carry):
            copy(step).start()
            return carry

        def finish(step, carry):
            copy(step).wait()
            return carry

        lax.fori_loop(1, sources, start, 0)
        return lambda: lax.fori_loop(1, sources, finish, 0)


    part_row = lax.broadcasted_iota(jnp.int32, (sources, 128), 0)
    group = lax.broadcasted_iota(jnp.int32, (sources, 128), 1) // 32
    seat = part_row % 4
    fold = jnp.where(
        lax.broadcasted_iota(jnp.int32, (blocks, sources), 0)
        == lax.broadcasted_iota(jnp.int32, (blocks, sources), 1) // 4,
        1.0,
        0.0,
    )
    unfold = jnp.where(
        lax.broadcasted_iota(jnp.int32, (sources, blocks), 0) // 4
        == lax.broadcasted_iota(jnp.int32, (sources, blocks), 1),
        1.0,
        0.0,
    )

    def exact(first, second):
        return jnp.dot(first, second, precision=lax.Precision.HIGHEST, preferred_element_type=f32)

    def dense(*seated):
        masked = [jnp.where(group == seat, value, 0.0) for value in seated]
        folded = exact(fold, jnp.concatenate(masked, axis=1))
        return [folded[:, i * 128 : (i + 1) * 128] for i in range(len(seated))]

    def four(value):
        return jnp.concatenate([value] * 4, axis=1)

    def as_row(value):
        return jnp.concatenate([value[b : b + 1] for b in range(blocks)], axis=1)

    def as_dense(value):
        return jnp.concatenate(
            [value[:, b * 128 : (b + 1) * 128] for b in range(blocks)], axis=0
        )

    counts = jnp.broadcast_to(count_ref[...].astype(f32), (sources, sources))
    diagonal = lax.broadcasted_iota(jnp.int32, (sources, sources), 0) == lax.broadcasted_iota(
        jnp.int32, (sources, sources), 1
    )
    count_column = jnp.sum(jnp.where(diagonal, counts, 0.0), axis=1, keepdims=True)
    slot_lane = (lax.broadcasted_iota(jnp.int32, (sources, 128), 1) % 32).astype(f32)
    live, rays, ranks = dense(
        jnp.where(slot_lane < count_column, 1.0, 0.0),
        four(ray_ref[...].astype(f32)),
        four(rank_ref[...].astype(f32)),
    )
    live = as_row(live)
    keys = rays * 64.0 + ranks
    key_row, rank_row = as_row(keys), as_row(ranks)
    key_column, ray_column = jnp.transpose(keys), jnp.transpose(rays)
    pl.semaphore_wait(barrier, sources + replicas - 2)
    wait_stats = exchange(stats_ref, stats_in, stats_send, stats_recv)
    own_stats = pltpu.make_async_copy(stats_ref.at[me], stats_in.at[me], local.at[2])
    own_stats.start()

    for chunk in range(blocks):
        gap = key_row - key_column[:, chunk : chunk + 1]
        ahead[pl.ds(chunk * 128, 128), :] = jnp.where(
            (gap > 0.5) & (gap < rank_row + 0.5), 1.0, 0.0
        ).astype(bf16)

    own_stats.wait()
    wait_stats()

    for index in range(sources):
        flat[pl.ds(index, 1), :] = stats_in[index, pl.ds(0, 1), :]
    packed = flat[...]
    turned = [packed] + [pltpu.roll(packed, 32 * step, 1) for step in range(1, 4)]

    def stat(index):
        value = turned[(3 - index) % 4]
        for place in range(3):
            value = jnp.where(seat == place, turned[(place - index) % 4], value)
        return value

    for index in range(sources):
        flat[pl.ds(index, 1), :] = stats_in[index, pl.ds(1, 1), :]
    sum_aa, sum_ab, sum_bb, log_prop, log_fine = (
        as_row(value) for value in dense(*(stat(index) for index in range(4)), flat[...])
    )

    def stacked(values):
        pieces = [piece.astype(f32) for value in values for piece in split_three(value)]
        pieces += [jnp.zeros_like(pieces[0])] * (8 - len(pieces))
        return jnp.concatenate(pieces, axis=0).astype(bf16)

    logs = stacked([log_prop * live, log_fine * live])
    reached = jnp.dot(logs, ahead[...], preferred_element_type=f32)
    entry_prop = jnp.exp(reached[0:1] + reached[1:2] + reached[2:3]) * live
    entry_fine = jnp.exp(reached[3:4] + reached[4:5] + reached[5:6]) * live
    slot_grad = distill_weight * (entry_prop * sum_aa - entry_fine * sum_ab) * entry_prop
    carried = lax.dot_general(
        stacked([slot_grad]), ahead[...], LANES_BOTH, preferred_element_type=f32
    )
    outgoing = (
        0.5 * distill_weight * entry_prop * entry_prop,
        -distill_weight * entry_prop * entry_fine,
        (carried[0:1] + carried[1:2] + carried[2:3]) * live,
    )
    message = jnp.zeros((sources, 128), f32)
    spreads = exact(unfold, jnp.concatenate([as_dense(value) for value in outgoing], axis=1))
    for index in range(len(outgoing)):
        spread = spreads[:, index * 128 : (index + 1) * 128]
        for place in range(4):
            shift = 32 * ((index - place) % 4)
            moved = pltpu.roll(spread, shift, 1) if shift else spread
            message = jnp.where((group == index) & (seat == place), moved, message)
    for index in range(sources):
        factors_out[index] = message[index : index + 1]

    wait_factors = exchange(factors_out, factors_in, factors_send, factors_recv)
    own_factors = pltpu.make_async_copy(factors_out.at[me], factors_in.at[me], local.at[3])
    own_factors.start()

    seg_loss = (
        entry_prop * entry_prop * sum_aa
        - 2.0 * entry_prop * entry_fine * sum_ab
        + entry_fine * entry_fine * sum_bb
    )
    losses = stacked([seg_loss])
    ray_loss = jnp.zeros((8, RAY_DEV), f32)
    ray_ids = lax.broadcasted_iota(jnp.int32, (128, RAY_DEV), 1).astype(f32)
    for chunk in range(blocks):
        mask = jnp.where(ray_column[:, chunk : chunk + 1] == ray_ids, 1.0, 0.0).astype(bf16)
        ray_loss = ray_loss + jnp.dot(
            losses[:, chunk * 128 : (chunk + 1) * 128], mask, preferred_element_type=f32
        )
    ray_loss = 0.5 * distill_weight * (ray_loss[0:1] + ray_loss[1:2] + ray_loss[2:3])
    for index in range(RAY_DEV // 128):
        result_ref[pl.ds(32 + index, 1), :] = ray_loss[:, index * 128 : (index + 1) * 128]

    load_back.wait()
    load_kept.wait()
    own_factors.wait()
    wait_factors()

    for index in range(sources):
        flat[pl.ds(index, 1), :] = factors_in[index]
    factors = flat[...]

    def to_samples(index):
        spread = group_total(jnp.where(group == index, factors, 0.0))
        return jnp.broadcast_to(spread[:, None, :], (sources, rows_per, 128)).reshape(
            sources * rows_per, 128
        )

    taken = back_ref[0]
    taken_grad = 2.0 * to_samples(0) * taken + to_samples(1) * back_ref[3]
    behind, unused = scan_segment(taken_grad * taken, rows_per, False)
    grad = (taken_grad * back_ref[1] - behind - to_samples(2)) * back_ref[2]
    logit_grad[...] = grad.astype(bf16).astype(f32)

    def accumulate(source, total):
        for part_index in range(rows_per):
            lanes = pl.ds(part_index * 128, 128)
            row = logit_grad[pl.ds(source * rows_per + part_index, 1), :]
            hidden = kept_ref[source, pl.ds(32, 16), lanes].astype(f32)
            wide = jnp.broadcast_to(row, (16, 128))
            left[pl.ds(0, 16), lanes] = jnp.where(hidden > 0, wide, 0.0).astype(bf16)
            left[pl.ds(16, 16), lanes] = wide.astype(bf16)
        return total + lax.dot_general(
            left[...], kept_ref[source], LANES_BOTH, preferred_element_type=f32
        )

    total = lax.fori_loop(0, sources, accumulate, jnp.zeros((32, rows_kept), f32))
    grads_in[replica] = jnp.concatenate([total, jnp.zeros((32, 128 - rows_kept), f32)], axis=1)

    def share(step):
        other = lax.rem(replica + step, replicas)
        return pltpu.make_async_remote_copy(
            src_ref=grads_in.at[replica],
            dst_ref=grads_in.at[replica],
            send_sem=grads_send.at[step],
            recv_sem=grads_recv.at[step],
            device_id=(me, other),
            device_id_type=MESH,
        )

    for step in range(1, replicas):
        share(step).start()
    for step in range(1, replicas):
        share(step).wait()
    summed = grads_in[0]
    for index in range(1, replicas):
        summed = summed + grads_in[index]
    head = jnp.broadcast_to(prop_out_ref[...].astype(f32), (16, 16))
    on_diagonal = lax.broadcasted_iota(jnp.int32, (16, 16), 0) == lax.broadcasted_iota(
        jnp.int32, (16, 16), 1
    )
    head_column = jnp.sum(jnp.where(on_diagonal, head, 0.0), axis=1, keepdims=True)
    result_ref[pl.ds(0, 16), :] = summed[0:16] * head_column
    result_ref[pl.ds(16, 16), :] = summed[16:32]


def split_kernel(result_ref, loss_ref, in_ref, out_ref):
    loss_ref[...] = result_ref[pl.ds(32, RAY_DEV // 128), :]
    in_ref[...] = result_ref[pl.ds(0, 16), :][:, 0:32]
    out_ref[...] = result_ref[pl.ds(16, 1), :][:, 32:48]


def vmem():
    return pl.BlockSpec(memory_space=pltpu.VMEM)


def on_device(
    feature_grid,
    fine_in,
    fine_mid,
    fine_out,
    prop_in,
    prop_out,
    sample_cells,
    sample_geometry,
    slot_ray,
    slot_rank,
    bucket_count,
):
    sources = lax.axis_size("dom")
    capacity = slot_ray.shape[3]
    width = sample_cells.shape[3]
    rows_all = sources * width // 128
    slots = sources * capacity
    cell_total = feature_grid.shape[2]
    params = pltpu.CompilerParams(vmem_limit_bytes=60 * 2**20)

    by_part = (
        sample_geometry.reshape(4, sources, width)
        .transpose(1, 0, 2)
        .reshape(sources, 4 * width // 128, 128)
    )
    geometry, corners = pl.pallas_call(
        scatter_kernel,
        out_shape=(
            jax.ShapeDtypeStruct(by_part.shape, f32),
            jax.ShapeDtypeStruct((cell_total, 128), bf16),
        ),
        in_specs=[vmem()] * 2,
        out_specs=(vmem(), pl.BlockSpec(memory_space=pl.ANY)),
        scratch_shapes=[
            pltpu.VMEM(by_part.shape, bf16),
            pltpu.VMEM((cell_total, 128), bf16),
            pltpu.SemaphoreType.DMA((sources,)),
            pltpu.SemaphoreType.DMA((sources,)),
            pltpu.SemaphoreType.DMA((PIECES + 1,)),
        ],
        compiler_params=pltpu.CompilerParams(
            vmem_limit_bytes=60 * 2**20, collective_id=1, has_side_effects=True
        ),
        name="scatter_geometry",
    )(by_part, feature_grid[0])
    kept, back, stats = pl.pallas_call(
        owner_kernel,
        out_shape=(
            jax.ShapeDtypeStruct((sources, 48, width), bf16),
            jax.ShapeDtypeStruct((4, rows_all, 128), f32),
            jax.ShapeDtypeStruct((sources, 2, 128), f32),
        ),
        in_specs=[pl.BlockSpec(memory_space=pl.ANY), vmem(), pl.BlockSpec(memory_space=pl.ANY)]
        + [vmem()] * 5,
        out_specs=(pl.BlockSpec(memory_space=pl.ANY), vmem(), vmem()),
        scratch_shapes=[
            pltpu.VMEM((sources, 48, width), bf16),
            pltpu.SemaphoreType.DMA((sources,)),
            pltpu.VMEM((cell_total, 128), bf16),
            pltpu.VMEM((2 * cell_total, 128), f32),
            pltpu.VMEM((2 * TILE, 128), f32),
            pltpu.VMEM((2 * TILE, 128), f32),
            pltpu.VMEM((rows_all, 128), f32),
            pltpu.VMEM((rows_all, 128), f32),
            pltpu.VMEM((rows_all, 128), f32),
            pltpu.SMEM((TILE,), jnp.int32),
            pltpu.SMEM((TILE,), jnp.int32),
            pltpu.SemaphoreType.DMA((2,)),
            pltpu.VMEM((TILE // PART * 80, TILE // PART * 32), bf16),
            pltpu.VMEM((fine_mid.shape[1], TILE // PART * 64, TILE // PART * 64), bf16),
            pltpu.VMEM((16, TILE // PART * 64), bf16),
            pltpu.VMEM((16, TILE // PART * 16), bf16),
            pltpu.VMEM((TILE // PART * 32, PART), bf16),
            pltpu.VMEM((TILE // PART * 32, PART), bf16),
        ],
        compiler_params=params,
        name="owner_forward",
    )(
        (sample_cells * 2).reshape(sources * width),
        geometry,
        corners,
        jnp.swapaxes(fine_in, 1, 2)[0],
        fine_mid[0],
        fine_out,
        prop_in[0],
        prop_out,
    )
    result = pl.pallas_call(
        finish_kernel,
        out_shape=jax.ShapeDtypeStruct((32 + RAY_DEV // 128, 128), f32),
        in_specs=[vmem()] * 5 + [pl.BlockSpec(memory_space=pl.ANY)] * 2,
        out_specs=vmem(),
        scratch_shapes=[
            pltpu.VMEM((sources, 2, 128), f32),
            pltpu.VMEM((sources, 1, 128), f32),
            pltpu.VMEM((sources, 1, 128), f32),
            pltpu.VMEM((lax.axis_size("rep"), 32, 128), f32),
            pltpu.VMEM((sources, 128), f32),
            pltpu.VMEM((slots, slots), bf16),
            pltpu.VMEM((rows_all, 128), f32),
            pltpu.VMEM((32, width), bf16),
            pltpu.VMEM((4, rows_all, 128), f32),
            pltpu.VMEM((sources, 48, width), bf16),
            pltpu.SemaphoreType.DMA((sources,)),
            pltpu.SemaphoreType.DMA((sources,)),
            pltpu.SemaphoreType.DMA((sources,)),
            pltpu.SemaphoreType.DMA((sources,)),
            pltpu.SemaphoreType.DMA((lax.axis_size("rep"),)),
            pltpu.SemaphoreType.DMA((lax.axis_size("rep"),)),
            pltpu.SemaphoreType.DMA((4,)),
        ],
        compiler_params=pltpu.CompilerParams(
            vmem_limit_bytes=58 * 2**20, collective_id=0, has_side_effects=True
        ),
        name="finish",
    )(
        stats,
        slot_ray[0, 0],
        slot_rank[0, 0],
        bucket_count[0],
        prop_out,
        back,
        kept,
    )
    ray_loss, in_grad, out_grad = pl.pallas_call(
        split_kernel,
        out_shape=(
            jax.ShapeDtypeStruct((RAY_DEV // 128, 128), f32),
            jax.ShapeDtypeStruct((16, 32), f32),
            jax.ShapeDtypeStruct((1, 16), f32),
        ),
        in_specs=[vmem()],
        out_specs=(vmem(), vmem(), vmem()),
        name="split",
    )(result)
    return (ray_loss.reshape(1, 1, RAY_DEV), in_grad[None], out_grad)


def solution(mesh):
    return jax.shard_map(
        on_device,
        mesh=mesh,
        in_specs=(
            P("dom", None, None),
            P("dom", None, None),
            P("dom", None, None, None),
            P("dom", None),
            P("dom", None, None),
            P("dom", None),
            P("dom", "rep", None, None),
            P(None, "dom", "rep", None, None),
            P("dom", "rep", None, None),
            P("dom", "rep", None, None),
            P("dom", "rep", None),
        ),
        out_specs=(P("dom", "rep", None), P("dom", None, None), P("dom", None)),
        check_vma=False,
    )
```
